256 devices in a mesh: ctx: 8 (over z), row: 2 (over core), exp: 16 (over x, y).
Axes of the slice: x: 4, y: 4, z: 8, core: 2. Of those that a mesh axis runs over, the one named last changes fastest.
Arguments:
- queries: bfloat16 [128, 128, 576], P(('row', 'exp')), may hold values from -10 to 10
- latent_cache: bfloat16 [128, 8192, 576], P(('row', 'exp'), 'ctx'), may hold values from -6 to 6
- lengths: int32 [128], P(('row', 'exp')), may hold values from 512 to 8192, as said below
- w_value: bfloat16 [128, 512, 128], P(('ctx', 'exp')), may hold values from -0.25 to 0.25
- w_out: bfloat16 [16384, 7168], P(('ctx', 'exp')), may hold values from -0.1875 to 0.1875
- stream: bfloat16 [128, 7168], P(('row', 'exp'), 'ctx'), may hold values from -6 to 6
- norm_gain: float32 [7168], P('ctx'), may hold values from 0.1 to 1.9
- expert_ids: int32 [128, 8], P(('row', 'exp')), may hold values from 0 to 31, all different within a row; in each aligned block of 4 rows (0 to 3, 4 to 7, ...) at most 2 rows name the same one
- gate_weights: float32 [128, 8], P(('row', 'exp')), may hold values from 0.1 to 0.6
- w_gate: bfloat16 [32, 7168, 1024], P(('row', 'exp'), 'ctx'), may hold values from -0.0625 to 0.0625
- w_up: bfloat16 [32, 7168, 1024], P(('row', 'exp'), 'ctx'), may hold values from -0.0625 to 0.0625
- w_down: bfloat16 [32, 1024, 7168], P(('row', 'exp'), None, 'ctx'), may hold values from -0.1875 to 0.1875
Outputs:
- layer_out: bfloat16 [128, 7168], P(('row', 'exp'), 'ctx')
The draws below stay inside these ranges and needn't reach their ends.
Inputs may be any that keep to these rules, and one draw needn't show every extreme that they name: `lengths`: some row has 8192 live positions and some row 512. `expert_ids`: each row names 8 different experts; among the 4 rows of one device no expert is named by more than 2 rows.
All inputs are finite; a program needn't handle non-finite values.
Results may differ from the reference program's by a relative error of at most 0.012.
Values may be sent and summed in bfloat16 or wider, within the bound.
No kernel may reach another device: no remote copies, remote signals or barrier semaphores. Data moves between devices by JAX's collectives and lax.ppermute only.
A program may use at most 64 MiB of HBM per device.

```python
import math
import jax
import jax.numpy as jnp
import numpy as np
from jax import lax

D = 7168
HEADS = 128
LAT = 512
ROPE = 64
QK_HEAD = 192
V_HEAD = 128
TOP = 8
FFE = 1024
ROW_GRP = 4
LENGTH = 8192
BLOCK = 1024
ROWS = 128
EXPERTS = 32
CAP = 2
N_CTX = 8


def draw_latent_cache(key, part):
    key = jax.random.fold_in(key, 7)
    shape = (ROWS, LENGTH, LAT + ROPE)
    base = jnp.clip(jax.random.normal(key, shape, jnp.float32), -6.0, 6.0)
    return base.astype(jnp.bfloat16)


def draw_queries(key, part):
    key = jax.random.fold_in(key, 9)
    shape = (ROWS, HEADS, LAT + ROPE)
    base = jnp.clip(jax.random.normal(key, shape, jnp.float32), -6.0, 6.0)
    return base.astype(jnp.bfloat16)


def draw_lengths(key, part):
    key = jax.random.fold_in(key, 5)
    drawn = jax.random.randint(key, (ROWS,), LENGTH // 16, LENGTH + 1)
    row_numbers = jnp.arange(ROWS)
    drawn = jnp.where(row_numbers == 0, LENGTH, drawn)
    drawn = jnp.where(row_numbers == 1, LENGTH // 16, drawn)
    return drawn.astype(jnp.int32)


def raised(entries, rng, source, target, parts, factor):
    def block_of(axis_at):
        return (jnp.arange(entries.shape[axis_at]) // (entries.shape[axis_at] // parts)).reshape((-1,) + (1,) * (entries.ndim - 1 - axis_at))

    one_side = jax.random.permutation(rng, parts)[block_of(target)]
    other_side = (block_of(target) + parts // 2) % parts
    return jnp.where((block_of(source) == one_side) | (block_of(source) == other_side), factor * entries, entries)


def shard_levels(rng, dims, shards, low, high):
    factor_of, own = 1.0, jax.random.fold_in(rng, 6)
    for dim, blocks in shards:
        draws = jnp.exp(jax.random.uniform(jax.random.fold_in(own, dim), (blocks,), jnp.float32, low / len(shards), high / len(shards)))
        factor_of = factor_of * jnp.repeat(draws, dims[dim] // blocks).reshape([-1 if axis == dim else 1 for axis in range(len(dims))])
    return factor_of


def routed_block(own_key, own, number, rows, count, top, bound, lean):
    ranking = jax.random.permutation(own_key, count)
    packed, usual = shares(count, rows * top, bound, lean, True), shares(count, rows * top, bound, lean, False)
    places = jnp.arange(count)

    def named(sizes, offset_by):
        used = int((sizes > 0).sum())
        fixed = max(1, used // 4)
        passed = fixed + (places - fixed + offset_by * (used - fixed)) % max(1, count - fixed)
        return jnp.zeros((count,), jnp.int32).at[ranking[jnp.where(places < fixed, places, passed)]].set(jnp.asarray(sizes, jnp.int32))

    sizes = jnp.where(number % 4 == 0, named(packed, number // 4), named(usual, number - number // 4 - 1))
    mixed = jax.random.permutation(jax.random.fold_in(own, 3), count)
    giver, sink = mixed[0:count // 2 * 2:2], mixed[1:count // 2 * 2:2]
    slack = jnp.minimum(sizes[giver] - 1, bound - sizes[sink]) // 2
    slack = jnp.where((giver == ranking[0]) | (sink == ranking[0]) | (sizes[sink] == 0), 0, jnp.maximum(slack, 0))
    passed = jax.random.randint(jax.random.fold_in(own, 4), (count // 2,), 0, 1 << 20) % (slack + 1)
    sizes = sizes.at[giver].add(-passed).at[sink].add(passed)
    labels = jnp.searchsorted(jnp.cumsum(sizes), jnp.arange(rows * top), side="right").astype(jnp.int32)
    grid = labels.reshape(top, rows).T
    grid = grid[jax.random.permutation(jax.random.fold_in(own, 1), rows)]
    offset_by = jax.random.randint(jax.random.fold_in(own, 2), (rows, 1), 0, top)
    return jnp.take_along_axis(grid, (jnp.arange(top)[None, :] + offset_by) % top, axis=1)


def shares(amount, total, most, lean, full):
    portions = [(1 << 20) // math.isqrt(grade ** lean) + 1 for grade in range(1, amount + 1)]
    largest = most if full else min(most, max(-(-total // amount), total * portions[0] // sum(portions)))
    least = 1 if total - largest >= amount - 1 else 0
    counts, spare = [largest] + [least] * (amount - 1), total - largest - least * (amount - 1)
    while spare > 0:
        movable = [i for i in range(1, amount) if counts[i] < largest] or [i for i in range(1, amount) if counts[i] < most]
        mass, left = sum([portions[i] for i in movable]), spare
        for i in movable:
            extra = min(most - counts[i], max(1, left * portions[i] // mass), spare)
            counts[i] = counts[i] + extra
            spare = spare - extra
    return np.array(counts)


def bell_draw(own_key, shape, scale, limit, pieces=(), kind=jnp.bfloat16):
    gain = shard_levels(own_key, shape, pieces, -0.22, 0.18) if pieces else 1.0
    values = jax.random.normal(own_key, shape, jnp.float32) * scale * gain
    return jnp.minimum(jnp.maximum(values, -limit), limit).astype(kind)


def heavy_noise(stream_key, shape, scale, most, shards, heavy, kind=jnp.bfloat16):
    entries = scale * jax.random.normal(stream_key, shape, jnp.float32)
    if shards:
        entries = entries * shard_levels(stream_key, shape, shards, -0.22, 0.18)
    return jnp.clip(raised(entries, jax.random.fold_in(stream_key, 3), *heavy), -most, most).astype(kind)


def setup_inputs(seed: int = 0) -> dict:
    splits = jax.random.split(jax.random.key(seed), 13)
    queries = draw_queries(jax.random.fold_in(splits[12], 71), 0)
    latent_cache = draw_latent_cache(jax.random.fold_in(splits[12], 71), 0)
    lengths = draw_lengths(jax.random.fold_in(splits[12], 71), 0)
    w_value = bell_draw(splits[3], (HEADS, LAT, V_HEAD), LAT ** -0.5, 0.25, ((0, 128),))
    w_out = heavy_noise(splits[4], (HEADS * V_HEAD, D), (HEADS * V_HEAD) ** -0.5, 0.1875, ((0, 128),), (0, 1, 128, 5.5))
    stream = bell_draw(splits[5], (ROWS, D), 1.0, 6.0, ((0, 32), (1, 8)))
    norm_gain = jnp.clip(1.0 + 0.18 * jax.random.normal(splits[6], (D,), jnp.float32), 0.1, 1.9)
    expert_ids_keys = jax.random.split(jax.random.fold_in(splits[7], 1), ROWS // ROW_GRP)
    expert_ids_turns = jax.random.permutation(jax.random.fold_in(splits[7], 3), ROWS // ROW_GRP)
    expert_ids = jax.vmap(lambda own, number: routed_block(jax.random.fold_in(splits[7], 2), own, number, ROW_GRP, EXPERTS, TOP, CAP, 2))(expert_ids_keys, expert_ids_turns).reshape((ROWS, TOP))
    gate_weights = jnp.clip(0.1 + 0.5 * jax.random.uniform(splits[8], (ROWS, TOP), jnp.float32) ** shard_levels(splits[8], (ROWS, TOP), ((0, 32),), -0.2, 0.2), 0.1, 0.6)
    w_gate = bell_draw(splits[9], (EXPERTS, D, FFE), D ** -0.5, 0.0625, ((0, 32), (1, 8)))
    w_up = bell_draw(splits[10], (EXPERTS, D, FFE), D ** -0.5, 0.0625, ((0, 32), (1, 8)))
    w_down = bell_draw(splits[11], (EXPERTS, FFE, D), FFE ** -0.5, 0.1875, ((0, 32), (2, 8)))
    return dict(queries=queries, latent_cache=latent_cache, lengths=lengths, w_value=w_value, w_out=w_out, stream=stream, norm_gain=norm_gain, expert_ids=expert_ids, gate_weights=gate_weights, w_gate=w_gate, w_up=w_up, w_down=w_down)


epsilon = 1e-06

def attend_row(inputs):
    query_row, cache_row, length = inputs
    scores = jnp.dot(query_row, cache_row.T, preferred_element_type=jnp.float32) * QK_HEAD ** (-0.5)
    scores = scores.reshape(HEADS, N_CTX, BLOCK)
    position = jnp.arange(LENGTH, dtype=jnp.int32).reshape(N_CTX, BLOCK)
    live = (position < length)[None]
    block_max = lax.optimization_barrier(jnp.max(jnp.where(live, scores, -jnp.inf), axis=2))
    shift_by = jnp.where(jnp.isfinite(block_max), block_max, 0.0)
    weights = jnp.where(live, jnp.exp(scores - shift_by[:, :, None]), 0.0)
    totals = lax.optimization_barrier(jnp.sum(weights, axis=2))
    weights_low = lax.optimization_barrier(weights.astype(jnp.bfloat16))
    latent_part = cache_row[:, :LAT].reshape(N_CTX, BLOCK, LAT)
    block_out = jnp.einsum('hcs,csl->hcl', weights_low.astype(jnp.float32), latent_part.astype(jnp.float32))
    top_value = lax.optimization_barrier(jnp.max(block_max, axis=1))
    factor = jnp.exp(block_max - top_value[:, None])
    numer = lax.optimization_barrier(jnp.sum(factor[:, :, None] * block_out, axis=1))
    denom = lax.optimization_barrier(jnp.sum(factor * totals, axis=1))
    return (numer / denom[:, None]).astype(jnp.bfloat16)

def reference(queries, latent_cache, lengths, w_value, w_out, stream, norm_gain, expert_ids, gate_weights, w_gate, w_up, w_down):
    attended = lax.map(attend_row, (queries, latent_cache, lengths))
    attended = lax.optimization_barrier(attended)
    values = jnp.einsum('bhl,hlv->bhv', attended.astype(jnp.float32), w_value.astype(jnp.float32))
    values = values.astype(jnp.bfloat16).reshape(ROWS, HEADS * V_HEAD)
    attn_out = jnp.dot(values, w_out, preferred_element_type=jnp.float32)
    hidden = lax.optimization_barrier((stream.astype(jnp.float32) + attn_out).astype(jnp.bfloat16))
    hidden_wide = hidden.astype(jnp.float32)
    inverse = lax.rsqrt(lax.optimization_barrier(jnp.sum(hidden_wide * hidden_wide, axis=1)) / D + epsilon)
    scaled = (hidden_wide * norm_gain[None, :]).astype(jnp.bfloat16)
    flat_ids = expert_ids.reshape(-1).astype(jnp.int32)
    row_index = jnp.arange(ROWS * TOP, dtype=jnp.int32) // TOP

    def expert_pair(inputs):
        row_at, expert_at = inputs
        vector = scaled[row_at]
        factor = inverse[row_at]
        gate_pre = factor * jnp.dot(vector, w_gate[expert_at], preferred_element_type=jnp.float32)
        up_pre = factor * jnp.dot(vector, w_up[expert_at], preferred_element_type=jnp.float32)
        active = (jax.nn.silu(gate_pre) * up_pre).astype(jnp.bfloat16)
        return jnp.dot(active, w_down[expert_at], preferred_element_type=jnp.float32).astype(jnp.bfloat16)
    produced = lax.map(expert_pair, (row_index, flat_ids))
    produced = lax.optimization_barrier(produced).reshape(ROWS, TOP, D)
    mixture = lax.optimization_barrier(jnp.sum(gate_weights[:, :, None] * produced.astype(jnp.float32), axis=1))
    return (hidden_wide + mixture).astype(jnp.bfloat16)
```

```python
import jax
import jax.numpy as jnp
from jax import lax
from jax.sharding import PartitionSpec as P

D = 7168
QK_HEAD = 192
BF = jnp.bfloat16
F32 = jnp.float32


epsilon = 1e-06


def exchange(x, axes):
    return lax.all_to_all(x, axes, split_axis=0, concat_axis=0, tiled=True)


def pieces(x):
    hi = x.astype(BF)
    rest = x - hi.astype(F32)
    mid = rest.astype(BF)
    low = (rest - mid.astype(F32)).astype(BF)
    return jnp.stack([hi, mid, low], axis=-1)


def on_device(
    queries,
    latent_cache,
    lengths,
    w_value,
    w_out,
    stream,
    norm_gain,
    expert_ids,
    gate_weights,
    w_gate,
    w_up,
    w_down,
):
    n_ctx = lax.axis_size("ctx")
    n_row = lax.axis_size("row")
    n_exp = lax.axis_size("exp")
    groups = queries.shape[0]
    heads = queries.shape[1]
    block = latent_cache.shape[1]
    latent = w_value.shape[1]
    width = stream.shape[1]
    scores = jnp.einsum(
        "bhw,btw->bht", queries, latent_cache, preferred_element_type=F32
    ) * QK_HEAD ** (-0.5)
    position = lax.axis_index("ctx") * block + jnp.arange(block, dtype=jnp.int32)
    live = (position[None, :] < lengths[:, None])[:, None, :]
    block_max = jnp.max(jnp.where(live, scores, -1e30), axis=2)
    weights = jnp.where(live, jnp.exp(scores - block_max[..., None]), 0.0)
    totals = jnp.sum(weights, axis=2)
    latent_out = jnp.einsum(
        "bht,btl->bhl", weights.astype(BF), latent_cache[:, :, :latent], preferred_element_type=F32
    )
    safe = jnp.where(totals > 0, totals, 1.0)
    lse = pieces(block_max + jnp.log(safe))
    per_ctx = heads // n_ctx
    part = (latent_out / safe[..., None]).astype(BF)
    part = part.reshape(groups, n_ctx, per_ctx, latent).transpose(1, 0, 2, 3)
    lse = lse.reshape(groups, n_ctx, per_ctx, 3).transpose(1, 0, 2, 3)
    lse = jnp.pad(lse.reshape(n_ctx, -1), ((0, 0), (0, 8 * latent - groups * per_ctx * 3)))
    sent = jnp.concatenate(
        [part.reshape(n_ctx, groups * per_ctx, latent), lse.reshape(n_ctx, 8, latent)], axis=1
    )
    got = exchange(sent, "ctx")
    lse = got[:, groups * per_ctx :].reshape(n_ctx, -1)[:, : groups * per_ctx * 3]
    lse = jnp.sum(lse.reshape(n_ctx, groups * per_ctx, 3).astype(F32), axis=-1)
    factor = jnp.exp(lse - jnp.max(lse, axis=0, keepdims=True))
    factor = factor / jnp.sum(factor, axis=0, keepdims=True)
    attended = jnp.sum(factor[..., None] * got[:, : groups * per_ctx].astype(F32), axis=0).astype(BF)
    attended = attended.reshape(groups, n_exp, latent).transpose(1, 0, 2)
    attended = exchange(attended.reshape(n_exp, groups * latent // 128, 128), "exp")
    gathered_rows = n_exp * groups
    attended = attended.reshape(gathered_rows, latent)
    values = jnp.dot(attended, w_value[0], preferred_element_type=F32).astype(BF)
    terms = jnp.dot(values, w_out, preferred_element_type=F32).astype(BF)
    terms = exchange(terms.reshape(n_exp, groups, D), "exp")
    terms = jnp.sum(terms.astype(F32), axis=0).astype(BF)
    terms = exchange(terms.reshape(groups, n_ctx, width).transpose(1, 0, 2), "ctx")
    attn_out = jnp.sum(terms.astype(F32), axis=0)
    hidden = lax.optimization_barrier((stream.astype(F32) + attn_out).astype(BF))
    experts = n_row * n_exp
    picks = expert_ids.shape[1]
    capacity = max(2, (groups * picks + experts - 1) // experts)
    expert_range = jnp.arange(experts, dtype=jnp.int32)
    onehot = expert_ids[:, :, None] == expert_range[None, None, :]
    named = jnp.sum(onehot.astype(jnp.int32), axis=1)
    slot_of = jnp.cumsum(named, axis=0) - named
    slot_match = slot_of[:, :, None] == jnp.arange(capacity, dtype=jnp.int32)[None, None, :]
    placed = (named[:, :, None] == 1) & slot_match
    outgoing = jnp.einsum("bxs,bd->xsd", placed.astype(BF), hidden, preferred_element_type=F32).astype(BF)
    arrived = exchange(outgoing, ("row", "exp")).reshape(experts * capacity, width)
    arrived_wide = arrived.astype(F32)
    sumsq = jnp.sum(arrived_wide * arrived_wide, axis=1)
    scaled = (arrived_wide * norm_gain[None, :]).astype(BF)
    gate_part = jnp.dot(scaled, w_gate[0], preferred_element_type=F32).astype(BF)
    up_part = jnp.dot(scaled, w_up[0], preferred_element_type=F32).astype(BF)
    extra = jnp.pad(pieces(sumsq), ((0, 0), (0, 125)))
    parts = jnp.concatenate([gate_part, up_part, extra], axis=1)
    per_dev = experts * capacity // n_ctx
    parts = exchange(parts.reshape(n_ctx, per_dev, parts.shape[1]), "ctx")
    sums = jnp.sum(parts.astype(F32), axis=0)
    hidden_units = w_gate.shape[2]
    gate_sum, up_sum = sums[:, :hidden_units], sums[:, hidden_units : 2 * hidden_units]
    sumsq = jnp.sum(sums[:, 2 * hidden_units : 2 * hidden_units + 3], axis=1)
    inverse = lax.rsqrt(sumsq / D + epsilon)[:, None]
    active = (jax.nn.silu(inverse * gate_sum) * (inverse * up_sum)).astype(BF)
    active = exchange(jnp.broadcast_to(active[None], (n_ctx,) + active.shape), "ctx")
    active = active.reshape(experts * capacity, hidden_units)
    produced = jnp.dot(active, w_down[0], preferred_element_type=F32).astype(BF)
    returned = exchange(produced.reshape(experts, capacity, width), ("row", "exp"))
    weighted = jnp.sum(gate_weights[:, :, None] * onehot.astype(F32), axis=1)
    combine = weighted[:, :, None] * slot_match.astype(F32)
    mixture = jnp.einsum("bxs,xsd->bd", combine, returned.astype(F32), precision=lax.Precision.HIGHEST)
    return (hidden.astype(F32) + mixture).astype(BF)


def solution(mesh):
    placed = (
        P(("row", "exp"), None, None),
        P(("row", "exp"), "ctx", None),
        P(("row", "exp")),
        P(("ctx", "exp"), None, None),
        P(("ctx", "exp"), None),
        P(("row", "exp"), "ctx"),
        P("ctx"),
        P(("row", "exp"), None),
        P(("row", "exp"), None),
        P(("row", "exp"), "ctx", None),
        P(("row", "exp"), "ctx", None),
        P(("row", "exp"), None, "ctx"),
    )
    return jax.shard_map(
        on_device, mesh=mesh, in_specs=placed, out_specs=P(("row", "exp"), "ctx"), check_vma=False
    )
```

```python
import functools

import jax
import jax.numpy as jnp
from jax import lax
from jax.experimental import pallas as pl
from jax.experimental.pallas import tpu as pltpu
from jax.sharding import PartitionSpec as P

D = 7168
QK_HEAD = 192
BF = jnp.bfloat16
F32 = jnp.float32
I32 = jnp.int32
epsilon = 1e-06
DEAD = -1e30
MIB = 1024 * 1024


def exchange(x, axes):
    return lax.all_to_all(x, axes, split_axis=0, concat_axis=0, tiled=True)


def dot(a, b, dims=((1,), (0,))):
    return lax.dot_general(a, b, (dims, ((), ())), preferred_element_type=F32)


def iota(shape, dim):
    return lax.broadcasted_iota(I32, shape, dim)


def pieces(x):
    hi = x.astype(BF).astype(F32)
    mid = (x - hi).astype(BF).astype(F32)
    low = (x - hi - mid).astype(BF).astype(F32)
    return hi, mid, low


def call(kernel, out, args, cost, **kw):
    return pl.pallas_call(
        kernel,
        out_shape=out,
        cost_estimate=pl.CostEstimate(flops=cost[0], bytes_accessed=cost[1], transcendentals=0),
        compiler_params=pltpu.CompilerParams(vmem_limit_bytes=24 * MIB),
        **kw,
    )(*args)


def shape_of(shape, dtype):
    return jax.ShapeDtypeStruct(shape, dtype)


def attend(live_ref, q_ref, kv_ref, out_ref, stat_ref):
    r = pl.program_id(0)
    n_ctx = out_ref.shape[0]
    heads, block = q_ref.shape[1], kv_ref.shape[1]
    latent = 512
    per = heads // n_ctx
    scores = dot(q_ref[0], kv_ref[0], ((1,), (1,))) * QK_HEAD ** (-0.5)
    live = iota((heads, block), 1) < live_ref[r]
    scores = jnp.where(live, scores, DEAD)
    top = jnp.max(scores, axis=1, keepdims=True)
    weights = jnp.where(live, jnp.exp(scores - top), 0.0)
    total = jnp.sum(weights, axis=1, keepdims=True)
    safe = jnp.where(total > 0, total, 1.0)
    part = dot(weights.astype(BF), kv_ref[0, :, :latent]) * (1.0 / safe)
    part = part.astype(BF)
    lane = iota((heads, 128), 1)

    @pl.when(r == 0)
    def _():
        stat_ref[...] = jnp.zeros_like(stat_ref)

    stat = stat_ref[...]
    for p, piece in enumerate(pieces(top + jnp.log(safe))):
        stat = jnp.where(lane == 4 * r + p, piece, stat)
    stat_ref[...] = stat
    tiles = latent // 128
    base = r * tiles * per
    for c in range(n_ctx):
        for t in range(tiles):
            at = pl.multiple_of(base + t * per, per)
            out_ref[c, pl.ds(at, per), :] = part[per * c : per * (c + 1), 128 * t : 128 * (t + 1)]

    @pl.when(r == pl.num_programs(0) - 1)
    def _():
        rows = pl.num_programs(0) * tiles * per
        for c in range(n_ctx):
            out_ref[c, pl.ds(rows, per), :] = stat[per * c : per * (c + 1)].astype(BF)


def merge(got_ref, out_ref):
    n_ctx, span, _ = got_ref.shape
    per = out_ref.shape[0]
    rows = 4
    tiles = (span - per) // per // rows
    stat = got_ref[:, span - per :, :].astype(F32)
    lane = iota(stat.shape, 2)
    merged = []
    for r in range(rows):
        mine = (lane >= 4 * r) & (lane < 4 * r + 3)
        lse = jnp.sum(jnp.where(mine, stat, 0.0), axis=2, keepdims=True)
        factor = jnp.exp(lse - jnp.max(lse, axis=0, keepdims=True))
        factor = factor * (1.0 / jnp.sum(factor, axis=0, keepdims=True))
        for t in range(tiles):
            at = (r * tiles + t) * per
            merged.append(jnp.sum(factor * got_ref[:, at : at + per, :].astype(F32), axis=0))
    merged = jnp.concatenate(merged, axis=0).astype(BF)
    size = rows * tiles * per
    i, j = iota((size, size), 0), iota((size, size), 1)
    n = rows * tiles
    swap = ((i // n == j % per) & (i % n == j // per)).astype(BF)
    out_ref[...] = dot(swap, merged).astype(BF).reshape(out_ref.shape)


def project(got_ref, wv_ref, wo_ref, out_ref):
    n_exp, n, _ = got_ref.shape
    rows = 4
    tiles = n // rows
    size = n_exp * n
    count = n_exp * rows
    i, j = iota((size, size), 0), iota((size, size), 1)
    t, b = i // count, i % count
    pick = (j == (b // rows) * n + (b % rows) * tiles + t).astype(BF)
    latents = dot(pick, got_ref[...].reshape(size, 128)).astype(BF)
    values = jnp.zeros((count, wv_ref.shape[2]), F32)
    for t in range(tiles):
        values += dot(latents[count * t : count * (t + 1)], wv_ref[0, 128 * t : 128 * (t + 1), :])
    values = values.astype(BF)
    i, j = iota((2 * count, count), 0), iota((2 * count, count), 1)
    double = (j == (i // 8) * rows + i % rows).astype(BF)
    doubled = dot(double, values)
    upper = (iota(doubled.shape, 0) // rows) % 2
    lhs = jnp.concatenate(
        [jnp.where(upper == 0, doubled, 0.0), jnp.where(upper == 1, doubled, 0.0)], axis=1
    ).astype(BF)
    half = wo_ref.shape[1] // 2
    step = 512
    for at in range(0, half, step):
        rhs = jnp.concatenate([wo_ref[:, at : at + step], wo_ref[:, half + at : half + at + step]], axis=0)
        out_ref[:, :, at : at + step] = dot(lhs, rhs).astype(BF).reshape(n_exp, 8, step)


def add_heads(got_ref, out_ref):
    n_ctx, rows, width = out_ref.shape
    per = n_ctx // 2
    for q in range(per):
        total = jnp.sum(got_ref[:, :, width * q : width * (q + 1)].astype(F32), axis=0)
        out_ref[q] = total[:rows]
        out_ref[per + q] = total[rows:]


def dispatch(got_ref, stream_ref, route_ref, hidden_ref, out_ref, scratch):
    rows, width = stream_ref.shape
    hidden = (stream_ref[...].astype(F32) + jnp.sum(got_ref[...], axis=0)).astype(BF)
    hidden_ref[...] = hidden
    wide = hidden.astype(F32)
    scratch[...] = jnp.zeros_like(scratch)
    for k in range(width // 128):
        scratch[8 * k : 8 * k + rows, :] = wide[:, 128 * k : 128 * (k + 1)]
    out_ref[...] = dot(route_ref[...], scratch[...].astype(BF)).astype(BF).reshape(out_ref.shape)


def routing(ids_ref, weights_ref, route_ref, combine_ref):
    size = route_ref.shape[0]
    rows, picks = ids_ref.shape
    i, j = iota((size, 64), 0), iota((size, 64), 1)
    expert, slot = i // 16, (i // 8) % 2
    same = (i % 8) == (j // 8)
    count = jnp.zeros((size, 64), I32)
    route = jnp.zeros((size, 64), F32)
    combine = jnp.zeros((size, 64), F32)
    for b in range(rows):
        weight = jnp.zeros((size, 64), F32)
        named = jnp.zeros((size, 64), I32)
        for k in range(picks):
            hit = expert == ids_ref[b, k]
            weight = jnp.where(hit, weights_ref[b, k], weight)
            named = jnp.where(hit, 1, named)
        mine = (named == 1) & (count == slot) & same & (j % 8 == b)
        route = jnp.where(mine, 1.0, route)
        combine = jnp.where(mine, weight, combine)
        count = count + named
    route_ref[...] = route.astype(BF)
    hi = combine.astype(BF)
    low = (combine - hi.astype(F32)).astype(BF)
    combine_ref[...] = jnp.concatenate([hi, low], axis=1)


def gate_up(got_ref, gain_ref, wg_ref, wu_ref, out_ref):
    n, span, _ = got_ref.shape
    slots = n * span // 8
    tiles = wg_ref.shape[1] // 128
    i, j = iota((tiles * slots, n * span), 0), iota((tiles * slots, n * span), 1)
    pick = ((j // 8 == i % slots) & (j % 8 == i // slots)).astype(BF)
    rows = dot(pick, got_ref[...].reshape(n * span, 128))
    sumsq = jnp.zeros((slots, 128), F32)
    scaled = []
    for k in range(tiles):
        part = rows[slots * k : slots * (k + 1)]
        sumsq += part * part
        scaled.append((part * gain_ref[:, 128 * k : 128 * (k + 1)]).astype(BF))
    scaled = jnp.concatenate(scaled, axis=1)
    units = wg_ref.shape[2]
    step = 512
    per = out_ref.shape[1]
    for w_ref, base in ((wg_ref, 0), (wu_ref, units)):
        for at in range(0, units, step):
            part = dot(scaled, w_ref[0, :, at : at + step]).astype(BF)
            out_ref[:, :, base + at : base + at + step] = part.reshape(slots // per, per, step)
    lane = iota((slots, 128), 1)
    stat = jnp.zeros((slots, 128), F32)
    for p, piece in enumerate(pieces(jnp.sum(sumsq, axis=1, keepdims=True))):
        stat = jnp.where(lane == p, piece, stat)
    out_ref[:, :, 2 * units :] = stat.astype(BF).reshape(slots // per, per, 128)


def activate(got_ref, out_ref):
    units = out_ref.shape[2]
    sums = jnp.sum(got_ref[...].astype(F32), axis=0)
    sumsq = jnp.sum(sums[:, 2 * units :], axis=1, keepdims=True)
    inverse = lax.rsqrt(sumsq / D + epsilon)
    gate = inverse * sums[:, :units]
    up = inverse * sums[:, units : 2 * units]
    active = (gate / (1.0 + jnp.exp(-gate)) * up).astype(BF)
    for c in range(out_ref.shape[0]):
        out_ref[c] = active


def down(got_ref, wd_ref, out_ref):
    n_ctx, per, units = got_ref.shape
    slots = n_ctx * per
    tiles = wd_ref.shape[2] // 128
    active = got_ref[...].reshape(slots, units)
    produced = dot(active, wd_ref[0]).astype(BF)
    stacked = jnp.concatenate([produced[:, 128 * k : 128 * (k + 1)] for k in range(tiles)], axis=0)
    size = slots * 8
    i, j = iota((size, tiles * slots), 0), iota((size, tiles * slots), 1)
    place = ((i // 8 == j % slots) & (i % 8 == j // slots)).astype(BF)
    out_ref[...] = dot(place, stacked).astype(BF).reshape(out_ref.shape)


def combine_rows(got_ref, combine_ref, hidden_ref, out_ref):
    rows, width = out_ref.shape
    n, span, _ = got_ref.shape
    mixed = dot(combine_ref[...], got_ref[...].reshape(n * span, 128), ((0,), (0,)))
    mixed = mixed[:64] + mixed[64:]
    for k in range(width // 128):
        at = slice(128 * k, 128 * (k + 1))
        out_ref[:, at] = (hidden_ref[:, at].astype(F32) + mixed[8 * k : 8 * k + rows]).astype(BF)


def on_device(
    queries,
    latent_cache,
    lengths,
    w_value,
    w_out,
    stream,
    norm_gain,
    expert_ids,
    gate_weights,
    w_gate,
    w_up,
    w_down,
):
    n_ctx = lax.axis_size("ctx")
    n_row = lax.axis_size("row")
    n_exp = lax.axis_size("exp")
    groups, heads, query_width = queries.shape
    block = latent_cache.shape[1]
    latent = w_value.shape[1]
    width = stream.shape[1]
    units = w_gate.shape[2]
    experts = n_row * n_exp
    slots = 2 * experts
    per = heads // n_ctx
    tiles = latent // 128
    span = groups * tiles * per + per

    route, combine = call(
        routing,
        (shape_of((slots * 8, 64), BF), shape_of((slots * 8, 128), BF)),
        (expert_ids, gate_weights),
        (slots * 8 * 64 * 100, slots * 8 * 400),
        in_specs=[pl.BlockSpec(memory_space=pltpu.SMEM)] * 2,
    )
    live = jnp.clip(lengths - lax.axis_index("ctx") * block, 0, block)
    sent = pl.pallas_call(
        attend,
        out_shape=shape_of((n_ctx, span, 128), BF),
        grid=(groups,),
        in_specs=[
            pl.BlockSpec(memory_space=pltpu.SMEM),
            pl.BlockSpec((1, heads, query_width), lambda r: (r, 0, 0)),
            pl.BlockSpec((1, block, query_width), lambda r: (r, 0, 0)),
        ],
        out_specs=pl.BlockSpec((n_ctx, span, 128), lambda r: (0, 0, 0)),
        scratch_shapes=[pltpu.VMEM((heads, 128), F32)],
        cost_estimate=pl.CostEstimate(
            flops=2 * groups * heads * block * (query_width + latent),
            bytes_accessed=2 * groups * (block + heads) * query_width,
            transcendentals=groups * heads * block,
        ),
        compiler_params=pltpu.CompilerParams(vmem_limit_bytes=24 * MIB),
    )(live, queries, latent_cache)
    got = exchange(sent, "ctx")
    sent = call(merge, shape_of((n_exp, groups * tiles, 128), BF), (got,), (1 << 22, 1 << 20))
    got = exchange(sent, "exp")
    sent = call(
        project,
        shape_of((n_exp, 2 * groups, D // 2), BF),
        (got, w_value, w_out),
        (2 * 128 * 256 * D // 2, 2 * 128 * D * 2),
    )
    got = exchange(sent, "exp")
    sent = call(add_heads, shape_of((n_ctx, groups, width), F32), (got,), (1 << 20, 1 << 20))
    got = exchange(sent, "ctx")
    hidden, sent = call(
        dispatch,
        (shape_of((groups, width), BF), shape_of((experts, 16, 128), BF)),
        (got, stream, route),
        (1 << 23, 1 << 19),
        scratch_shapes=[pltpu.VMEM((64, 128), F32)],
    )
    got = exchange(sent, ("row", "exp"))
    sent = call(
        gate_up,
        shape_of((n_ctx, slots // n_ctx, 2 * units + 128), BF),
        (got, norm_gain.reshape(1, width), w_gate, w_up),
        (4 * slots * width * units, 4 * width * units),
    )
    got = exchange(sent, "ctx")
    sent = call(activate, shape_of((n_ctx, slots // n_ctx, units), BF), (got,), (1 << 20, 1 << 19))
    got = exchange(sent, "ctx")
    sent = call(
        down,
        shape_of((experts, 16, 128), BF),
        (got, w_down),
        (2 * slots * width * units, 2 * width * units),
    )
    got = exchange(sent, ("row", "exp"))
    return call(
        combine_rows, shape_of((groups, width), BF), (got, combine, hidden), (1 << 24, 1 << 18)
    )


def solution(mesh):
    placed = (
        P(("row", "exp"), None, None),
        P(("row", "exp"), "ctx", None),
        P(("row", "exp")),
        P(("ctx", "exp"), None, None),
        P(("ctx", "exp"), None),
        P(("row", "exp"), "ctx"),
        P("ctx"),
        P(("row", "exp"), None),
        P(("row", "exp"), None),
        P(("row", "exp"), "ctx", None),
        P(("row", "exp"), "ctx", None),
        P(("row", "exp"), None, "ctx"),
    )
    return jax.shard_map(
        on_device, mesh=mesh, in_specs=placed, out_specs=P(("row", "exp"), "ctx"), check_vma=False
    )
```

```python
import functools

import jax
import jax.numpy as jnp
from jax import lax
from jax.experimental import pallas as pl
from jax.experimental.pallas import tpu as pltpu
from jax.sharding import PartitionSpec as P

D = 7168
QK_HEAD = 192
BF = jnp.bfloat16
F32 = jnp.float32
I32 = jnp.int32
epsilon = 1e-06
DEAD = -1e30
MIB = 1024 * 1024


def exchange(x, axes):
    return lax.all_to_all(x, axes, split_axis=0, concat_axis=0, tiled=True)


def dot(a, b, dims=((1,), (0,))):
    return lax.dot_general(a, b, (dims, ((), ())), preferred_element_type=F32)


def iota(shape, dim):
    return lax.broadcasted_iota(I32, shape, dim)


def pieces(x):
    hi = x.astype(BF).astype(F32)
    mid = (x - hi).astype(BF).astype(F32)
    low = (x - hi - mid).astype(BF).astype(F32)
    return hi, mid, low


def call(kernel, out, args, cost, **kw):
    return pl.pallas_call(
        kernel,
        out_shape=out,
        cost_estimate=pl.CostEstimate(flops=cost[0], bytes_accessed=cost[1], transcendentals=0),
        compiler_params=pltpu.CompilerParams(vmem_limit_bytes=24 * MIB),
        **kw,
    )(*args)


def shape_of(shape, dtype):
    return jax.ShapeDtypeStruct(shape, dtype)


def attend(live_ref, q_ref, kv_ref, out_ref, stat_ref):
    r = pl.program_id(0)
    n_ctx = out_ref.shape[0]
    heads, block = q_ref.shape[2], kv_ref.shape[2]
    latent = 512
    per = heads // n_ctx
    scores = dot(q_ref[0], kv_ref[0], ((0,), (0,))) * QK_HEAD ** (-0.5)
    live = iota((heads, block), 1) < live_ref[r]
    scores = jnp.where(live, scores, DEAD)
    top = jnp.max(scores, axis=1, keepdims=True)
    weights = jnp.where(live, jnp.exp(scores - top), 0.0)
    total = jnp.sum(weights, axis=1, keepdims=True)
    safe = jnp.where(total > 0, total, 1.0)
    part = dot(weights.astype(BF), kv_ref[0, :latent, :], ((1,), (1,))) * (1.0 / safe)
    part = part.astype(BF)
    lane = iota((heads, 128), 1)

    @pl.when(r == 0)
    def _():
        stat_ref[...] = jnp.zeros_like(stat_ref)

    stat = stat_ref[...]
    for p, piece in enumerate(pieces(top + jnp.log(safe))):
        stat = jnp.where(lane == 4 * r + p, piece, stat)
    stat_ref[...] = stat
    tiles = latent // 128
    base = r * tiles * per
    for c in range(n_ctx):
        for t in range(tiles):
            at = pl.multiple_of(base + t * per, per)
            out_ref[c, pl.ds(at, per), :] = part[per * c : per * (c + 1), 128 * t : 128 * (t + 1)]

    @pl.when(r == pl.num_programs(0) - 1)
    def _():
        rows = pl.num_programs(0) * tiles * per
        for c in range(n_ctx):
            out_ref[c, pl.ds(rows, per), :] = stat[per * c : per * (c + 1)].astype(BF)


def merge(got_ref, out_ref):
    n_ctx, span, _ = got_ref.shape
    per = out_ref.shape[0]
    rows = 4
    tiles = (span - per) // per // rows
    stat = got_ref[:, span - per :, :].astype(F32)
    lane = iota(stat.shape, 2)
    merged = []
    for r in range(rows):
        mine = (lane >= 4 * r) & (lane < 4 * r + 3)
        lse = jnp.sum(jnp.where(mine, stat, 0.0), axis=2, keepdims=True)
        factor = jnp.exp(lse - jnp.max(lse, axis=0, keepdims=True))
        factor = factor * (1.0 / jnp.sum(factor, axis=0, keepdims=True))
        for t in range(tiles):
            at = (r * tiles + t) * per
            merged.append(jnp.sum(factor * got_ref[:, at : at + per, :].astype(F32), axis=0))
    merged = jnp.concatenate(merged, axis=0).astype(BF)
    size = rows * tiles * per
    i, j = iota((size, size), 0), iota((size, size), 1)
    n = rows * tiles
    swap = ((i // n == j % per) & (i % n == j // per)).astype(BF)
    out_ref[...] = dot(swap, merged).astype(BF).reshape(out_ref.shape)


def project(got_ref, wv_ref, wo_ref, out_ref):
    n_exp, n, _ = got_ref.shape
    rows = 4
    tiles = n // rows
    size = n_exp * n
    count = n_exp * rows
    i, j = iota((size, size), 0), iota((size, size), 1)
    t, b = i // count, i % count
    pick = (j == (b // rows) * n + (b % rows) * tiles + t).astype(BF)
    latents = dot(pick, got_ref[...].reshape(size, 128)).astype(BF)
    values = jnp.zeros((count, wv_ref.shape[2]), F32)
    for t in range(tiles):
        values += dot(latents[count * t : count * (t + 1)], wv_ref[0, 128 * t : 128 * (t + 1), :])
    values = values.astype(BF)
    i, j = iota((2 * count, count), 0), iota((2 * count, count), 1)
    double = (j == (i // 8) * rows + i % rows).astype(BF)
    doubled = dot(double, values)
    upper = (iota(doubled.shape, 0) // rows) % 2
    lhs = jnp.concatenate(
        [jnp.where(upper == 0, doubled, 0.0), jnp.where(upper == 1, doubled, 0.0)], axis=1
    ).astype(BF)
    half = wo_ref.shape[1] // 2
    step = 512
    for at in range(0, half, step):
        rhs = jnp.concatenate([wo_ref[:, at : at + step], wo_ref[:, half + at : half + at + step]], axis=0)
        out_ref[:, :, at : at + step] = dot(lhs, rhs).astype(BF).reshape(n_exp, 8, step)


def add_heads(got_ref, out_ref):
    n_ctx, rows, width = out_ref.shape
    per = n_ctx // 2
    for q in range(per):
        total = jnp.sum(got_ref[:, :, width * q : width * (q + 1)].astype(F32), axis=0)
        out_ref[q] = total[:rows]
        out_ref[per + q] = total[rows:]


def dispatch(got_ref, stream_ref, route_ref, hidden_ref, out_ref, scratch):
    rows, width = stream_ref.shape
    hidden = (stream_ref[...].astype(F32) + jnp.sum(got_ref[...], axis=0)).astype(BF)
    hidden_ref[...] = hidden
    wide = hidden.astype(F32)
    scratch[...] = jnp.zeros_like(scratch)
    for k in range(width // 128):
        scratch[8 * k : 8 * k + rows, :] = wide[:, 128 * k : 128 * (k + 1)]
    out_ref[...] = dot(route_ref[...], scratch[...].astype(BF)).astype(BF).reshape(out_ref.shape)


def routing(ids_ref, weights_ref, route_ref, combine_ref):
    size = route_ref.shape[0]
    rows, picks = ids_ref.shape
    i, j = iota((size, 64), 0), iota((size, 64), 1)
    expert, slot = i // 16, (i // 8) % 2
    same = (i % 8) == (j // 8)
    count = jnp.zeros((size, 64), I32)
    route = jnp.zeros((size, 64), F32)
    combine = jnp.zeros((size, 64), F32)
    for b in range(rows):
        weight = jnp.zeros((size, 64), F32)
        named = jnp.zeros((size, 64), I32)
        for k in range(picks):
            hit = expert == ids_ref[b, k]
            weight = jnp.where(hit, weights_ref[b, k], weight)
            named = jnp.where(hit, 1, named)
        mine = (named == 1) & (count == slot) & same & (j % 8 == b)
        route = jnp.where(mine, 1.0, route)
        combine = jnp.where(mine, weight, combine)
        count = count + named
    route_ref[...] = route.astype(BF)
    hi = combine.astype(BF)
    low = (combine - hi.astype(F32)).astype(BF)
    combine_ref[...] = jnp.concatenate([hi, low], axis=1)


def gate_up(got_ref, gain_ref, wg_ref, wu_ref, out_ref):
    n, span, _ = got_ref.shape
    slots = n * span // 8
    tiles = wg_ref.shape[1] // 128
    i, j = iota((tiles * slots, n * span), 0), iota((tiles * slots, n * span), 1)
    pick = ((j // 8 == i % slots) & (j % 8 == i // slots)).astype(BF)
    rows = dot(pick, got_ref[...].reshape(n * span, 128))
    sumsq = jnp.zeros((slots, 128), F32)
    scaled = []
    for k in range(tiles):
        part = rows[slots * k : slots * (k + 1)]
        sumsq += part * part
        scaled.append((part * gain_ref[:, 128 * k : 128 * (k + 1)]).astype(BF))
    scaled = jnp.concatenate(scaled, axis=1)
    units = wg_ref.shape[2]
    step = 512
    per = out_ref.shape[1]
    for w_ref, base in ((wg_ref, 0), (wu_ref, units)):
        for at in range(0, units, step):
            part = dot(scaled, w_ref[0, :, at : at + step]).astype(BF)
            out_ref[:, :, base + at : base + at + step] = part.reshape(slots // per, per, step)
    lane = iota((slots, 128), 1)
    stat = jnp.zeros((slots, 128), F32)
    for p, piece in enumerate(pieces(jnp.sum(sumsq, axis=1, keepdims=True))):
        stat = jnp.where(lane == p, piece, stat)
    out_ref[:, :, 2 * units :] = stat.astype(BF).reshape(slots // per, per, 128)


def activate(got_ref, out_ref):
    units = out_ref.shape[2]
    sums = jnp.sum(got_ref[...].astype(F32), axis=0)
    sumsq = jnp.sum(sums[:, 2 * units :], axis=1, keepdims=True)
    inverse = lax.rsqrt(sumsq / D + epsilon)
    gate = inverse * sums[:, :units]
    up = inverse * sums[:, units : 2 * units]
    active = (gate / (1.0 + jnp.exp(-gate)) * up).astype(BF)
    for c in range(out_ref.shape[0]):
        out_ref[c] = active


def down(got_ref, wd_ref, out_ref):
    n_ctx, per, units = got_ref.shape
    slots = n_ctx * per
    tiles = wd_ref.shape[2] // 128
    active = got_ref[...].reshape(slots, units)
    produced = dot(active, wd_ref[0]).astype(BF)
    stacked = jnp.concatenate([produced[:, 128 * k : 128 * (k + 1)] for k in range(tiles)], axis=0)
    size = slots * 8
    i, j = iota((size, tiles * slots), 0), iota((size, tiles * slots), 1)
    place = ((i // 8 == j % slots) & (i % 8 == j // slots)).astype(BF)
    out_ref[...] = dot(place, stacked).astype(BF).reshape(out_ref.shape)


def combine_rows(got_ref, combine_ref, hidden_ref, out_ref):
    rows, width = out_ref.shape
    n, span, _ = got_ref.shape
    mixed = dot(combine_ref[...], got_ref[...].reshape(n * span, 128), ((0,), (0,)))
    mixed = mixed[:64] + mixed[64:]
    for k in range(width // 128):
        at = slice(128 * k, 128 * (k + 1))
        out_ref[:, at] = (hidden_ref[:, at].astype(F32) + mixed[8 * k : 8 * k + rows]).astype(BF)


def on_device(
    queries,
    latent_cache,
    lengths,
    w_value,
    w_out,
    stream,
    norm_gain,
    expert_ids,
    gate_weights,
    w_gate,
    w_up,
    w_down,
):
    n_ctx = lax.axis_size("ctx")
    n_row = lax.axis_size("row")
    n_exp = lax.axis_size("exp")
    groups, heads, query_width = queries.shape
    block = latent_cache.shape[1]
    latent = w_value.shape[1]
    width = stream.shape[1]
    units = w_gate.shape[2]
    experts = n_row * n_exp
    slots = 2 * experts
    per = heads // n_ctx
    tiles = latent // 128
    span = groups * tiles * per + per

    route, combine = call(
        routing,
        (shape_of((slots * 8, 64), BF), shape_of((slots * 8, 128), BF)),
        (expert_ids, gate_weights),
        (slots * 8 * 64 * 100, slots * 8 * 400),
        in_specs=[pl.BlockSpec(memory_space=pltpu.SMEM)] * 2,
    )
    live = jnp.clip(lengths - lax.axis_index("ctx") * block, 0, block)
    sent = pl.pallas_call(
        attend,
        out_shape=shape_of((n_ctx, span, 128), BF),
        grid=(groups,),
        in_specs=[
            pl.BlockSpec(memory_space=pltpu.SMEM),
            pl.BlockSpec((1, query_width, heads), lambda r: (r, 0, 0)),
            pl.BlockSpec((1, query_width, block), lambda r: (r, 0, 0)),
        ],
        out_specs=pl.BlockSpec((n_ctx, span, 128), lambda r: (0, 0, 0)),
        scratch_shapes=[pltpu.VMEM((heads, 128), F32)],
        cost_estimate=pl.CostEstimate(
            flops=2 * groups * heads * block * (query_width + latent),
            bytes_accessed=2 * groups * (block + heads) * query_width,
            transcendentals=groups * heads * block,
        ),
        compiler_params=pltpu.CompilerParams(vmem_limit_bytes=24 * MIB),
    )(live, jnp.swapaxes(queries, 1, 2), jnp.swapaxes(latent_cache, 1, 2))
    got = exchange(sent, "ctx")
    sent = call(merge, shape_of((n_exp, groups * tiles, 128), BF), (got,), (1 << 22, 1 << 20))
    got = exchange(sent, "exp")
    sent = call(
        project,
        shape_of((n_exp, 2 * groups, D // 2), BF),
        (got, w_value, w_out),
        (2 * 128 * 256 * D // 2, 2 * 128 * D * 2),
    )
    got = exchange(sent, "exp")
    sent = call(add_heads, shape_of((n_ctx, groups, width), F32), (got,), (1 << 20, 1 << 20))
    got = exchange(sent, "ctx")
    hidden, sent = call(
        dispatch,
        (shape_of((groups, width), BF), shape_of((experts, 16, 128), BF)),
        (got, stream, route),
        (1 << 23, 1 << 19),
        scratch_shapes=[pltpu.VMEM((64, 128), F32)],
    )
    got = exchange(sent, ("row", "exp"))
    sent = call(
        gate_up,
        shape_of((n_ctx, slots // n_ctx, 2 * units + 128), BF),
        (got, norm_gain.reshape(1, width), w_gate, w_up),
        (4 * slots * width * units, 4 * width * units),
    )
    got = exchange(sent, "ctx")
    sent = call(activate, shape_of((n_ctx, slots // n_ctx, units), BF), (got,), (1 << 20, 1 << 19))
    got = exchange(sent, "ctx")
    sent = call(
        down,
        shape_of((experts, 16, 128), BF),
        (got, w_down),
        (2 * slots * width * units, 2 * width * units),
    )
    got = exchange(sent, ("row", "exp"))
    return call(
        combine_rows, shape_of((groups, width), BF), (got, combine, hidden), (1 << 24, 1 << 18)
    )


def solution(mesh):
    placed = (
        P(("row", "exp"), None, None),
        P(("row", "exp"), "ctx", None),
        P(("row", "exp")),
        P(("ctx", "exp"), None, None),
        P(("ctx", "exp"), None),
        P(("row", "exp"), "ctx"),
        P("ctx"),
        P(("row", "exp"), None),
        P(("row", "exp"), None),
        P(("row", "exp"), "ctx", None),
        P(("row", "exp"), "ctx", None),
        P(("row", "exp"), None, "ctx"),
    )
    return jax.shard_map(
        on_device, mesh=mesh, in_specs=placed, out_specs=P(("row", "exp"), "ctx"), check_vma=False
    )
```

```python
import functools

import jax
import jax.numpy as jnp
from jax import lax
from jax.experimental import pallas as pl
from jax.experimental.pallas import tpu as pltpu
from jax.sharding import PartitionSpec as P

D = 7168
QK_HEAD = 192
BF = jnp.bfloat16
F32 = jnp.float32
I32 = jnp.int32
epsilon = 1e-06
DEAD = -1e30
MIB = 1024 * 1024


def exchange(x, axes):
    return lax.all_to_all(x, axes, split_axis=0, concat_axis=0, tiled=True)


def dot(a, b, dims=((1,), (0,))):
    return lax.dot_general(a, b, (dims, ((), ())), preferred_element_type=F32)


def iota(shape, dim):
    return lax.broadcasted_iota(I32, shape, dim)


def pieces(x):
    hi = x.astype(BF).astype(F32)
    mid = (x - hi).astype(BF).astype(F32)
    low = (x - hi - mid).astype(BF).astype(F32)
    return hi, mid, low


def call(kernel, out, args, cost, **kw):
    return pl.pallas_call(
        kernel,
        out_shape=out,
        cost_estimate=pl.CostEstimate(flops=cost[0], bytes_accessed=cost[1], transcendentals=0),
        compiler_params=pltpu.CompilerParams(vmem_limit_bytes=24 * MIB),
        **kw,
    )(*args)


def shape_of(shape, dtype):
    return jax.ShapeDtypeStruct(shape, dtype)


def attend(length_hbm, q_hbm, kv_hbm, out_ref, q_ref, kv_ref, length_ref, sem, length_sem):
    rows, _, heads = q_ref.shape
    block = kv_ref.shape[2]
    n_ctx, span, _ = out_ref.shape
    per = heads // n_ctx
    tiles = (span - per) // per // rows
    latent = tiles * 128
    copies = []
    for r in range(rows):
        pair = (
            pltpu.make_async_copy(q_hbm.at[r], q_ref.at[r], sem.at[0, r]),
            pltpu.make_async_copy(kv_hbm.at[r], kv_ref.at[r], sem.at[1, r]),
        )
        for copy in pair:
            copy.start()
        copies.append(pair)
    length_copy = pltpu.make_async_copy(length_hbm, length_ref, length_sem)
    length_copy.start()
    length_copy.wait()
    first = lax.axis_index("ctx") * block
    lane = iota((heads, 128), 1)
    stat = jnp.zeros((heads, 128), F32)
    for r in range(rows):
        for copy in copies[r]:
            copy.wait()
        scores = dot(q_ref[r], kv_ref[r], ((0,), (0,))) * QK_HEAD ** (-0.5)
        live = iota((heads, block), 1) < length_ref[r] - first
        scores = jnp.where(live, scores, DEAD)
        top = jnp.max(scores, axis=1, keepdims=True)
        weights = jnp.where(live, jnp.exp(scores - top), 0.0)
        total = jnp.sum(weights, axis=1, keepdims=True)
        safe = jnp.where(total > 0, total, 1.0)
        part = dot(weights.astype(BF), kv_ref[r, :latent, :], ((1,), (1,))) * (1.0 / safe)
        part = part.astype(BF)
        for p, piece in enumerate(pieces(top + jnp.log(safe))):
            stat = jnp.where(lane == 4 * r + p, piece, stat)
        for c in range(n_ctx):
            for t in range(tiles):
                at = (r * tiles + t) * per
                out_ref[c, at : at + per, :] = part[per * c : per * (c + 1), 128 * t : 128 * (t + 1)]
    stat = stat.astype(BF)
    for c in range(n_ctx):
        out_ref[c, span - per :, :] = stat[per * c : per * (c + 1)]


def merge(got_ref, out_ref):
    n_ctx, span, _ = got_ref.shape
    per = out_ref.shape[0]
    rows = 4
    tiles = (span - per) // per // rows
    stat = got_ref[:, span - per :, :].astype(F32)
    lane = iota(stat.shape, 2)
    merged = []
    for r in range(rows):
        mine = (lane >= 4 * r) & (lane < 4 * r + 3)
        lse = jnp.sum(jnp.where(mine, stat, 0.0), axis=2, keepdims=True)
        factor = jnp.exp(lse - jnp.max(lse, axis=0, keepdims=True))
        factor = factor * (1.0 / jnp.sum(factor, axis=0, keepdims=True))
        for t in range(tiles):
            at = (r * tiles + t) * per
            merged.append(jnp.sum(factor * got_ref[:, at : at + per, :].astype(F32), axis=0))
    merged = jnp.concatenate(merged, axis=0).astype(BF)
    size = rows * tiles * per
    i, j = iota((size, size), 0), iota((size, size), 1)
    n = rows * tiles
    swap = ((i // n == j % per) & (i % n == j // per)).astype(BF)
    out_ref[...] = dot(swap, merged).astype(BF).reshape(out_ref.shape)


def project(got_ref, wv_ref, wo_ref, out_ref):
    n_exp, n, _ = got_ref.shape
    rows = 4
    tiles = n // rows
    size = n_exp * n
    count = n_exp * rows
    i, j = iota((size, size), 0), iota((size, size), 1)
    t, b = i // count, i % count
    pick = (j == (b // rows) * n + (b % rows) * tiles + t).astype(BF)
    latents = dot(pick, got_ref[...].reshape(size, 128)).astype(BF)
    values = jnp.zeros((count, wv_ref.shape[2]), F32)
    for t in range(tiles):
        values += dot(latents[count * t : count * (t + 1)], wv_ref[0, 128 * t : 128 * (t + 1), :])
    values = values.astype(BF)
    i, j = iota((2 * count, count), 0), iota((2 * count, count), 1)
    double = (j == (i // 8) * rows + i % rows).astype(BF)
    doubled = dot(double, values)
    upper = (iota(doubled.shape, 0) // rows) % 2
    lhs = jnp.concatenate(
        [jnp.where(upper == 0, doubled, 0.0), jnp.where(upper == 1, doubled, 0.0)], axis=1
    ).astype(BF)
    half = wo_ref.shape[1] // 2
    step = 512
    for at in range(0, half, step):
        rhs = jnp.concatenate([wo_ref[:, at : at + step], wo_ref[:, half + at : half + at + step]], axis=0)
        out_ref[:, :, at : at + step] = dot(lhs, rhs).astype(BF).reshape(n_exp, 8, step)


def add_heads(got_ref, out_ref):
    n_ctx, rows, width = out_ref.shape
    per = n_ctx // 2
    for q in range(per):
        total = jnp.sum(got_ref[:, :, width * q : width * (q + 1)].astype(F32), axis=0)
        out_ref[q] = total[:rows].astype(BF)
        out_ref[per + q] = total[rows:].astype(BF)


def dispatch(got_ref, stream_ref, route_ref, hidden_ref, out_ref, scratch):
    rows, width = stream_ref.shape
    hidden = (stream_ref[...].astype(F32) + jnp.sum(got_ref[...].astype(F32), axis=0)).astype(BF)
    hidden_ref[...] = hidden
    wide = hidden.astype(F32)
    scratch[...] = jnp.zeros_like(scratch)
    for k in range(width // 128):
        scratch[8 * k : 8 * k + rows, :] = wide[:, 128 * k : 128 * (k + 1)]
    out_ref[...] = dot(route_ref[...], scratch[...].astype(BF)).astype(BF).reshape(out_ref.shape)


def routing(ids_ref, weights_ref, route_ref, combine_ref):
    size = route_ref.shape[0]
    rows, picks = ids_ref.shape
    i, j = iota((size, 64), 0), iota((size, 64), 1)
    expert, slot = i // 16, (i // 8) % 2
    same = (i % 8) == (j // 8)
    count = jnp.zeros((size, 64), I32)
    route = jnp.zeros((size, 64), F32)
    combine = jnp.zeros((size, 64), F32)
    for b in range(rows):
        weight = jnp.zeros((size, 64), F32)
        named = jnp.zeros((size, 64), I32)
        for k in range(picks):
            hit = expert == ids_ref[b, k]
            weight = jnp.where(hit, weights_ref[b, k], weight)
            named = jnp.where(hit, 1, named)
        mine = (named == 1) & (count == slot) & same & (j % 8 == b)
        route = jnp.where(mine, 1.0, route)
        combine = jnp.where(mine, weight, combine)
        count = count + named
    route_ref[...] = route.astype(BF)
    hi = combine.astype(BF)
    low = (combine - hi.astype(F32)).astype(BF)
    combine_ref[...] = jnp.concatenate([hi, low], axis=1)


def gate_up(got_ref, gain_ref, wg_ref, wu_ref, out_ref):
    n, span, _ = got_ref.shape
    slots = n * span // 8
    tiles = wg_ref.shape[1] // 128
    i, j = iota((tiles * slots, n * span), 0), iota((tiles * slots, n * span), 1)
    pick = ((j // 8 == i % slots) & (j % 8 == i // slots)).astype(BF)
    rows = dot(pick, got_ref[...].reshape(n * span, 128))
    sumsq = jnp.zeros((slots, 128), F32)
    scaled = []
    for k in range(tiles):
        part = rows[slots * k : slots * (k + 1)]
        sumsq += part * part
        scaled.append((part * gain_ref[:, 128 * k : 128 * (k + 1)]).astype(BF))
    scaled = jnp.concatenate(scaled, axis=1)
    units = wg_ref.shape[2]
    step = 512
    per = out_ref.shape[1]
    for w_ref, base in ((wg_ref, 0), (wu_ref, units)):
        for at in range(0, units, step):
            part = dot(scaled, w_ref[0, :, at : at + step]).astype(BF)
            out_ref[:, :, base + at : base + at + step] = part.reshape(slots // per, per, step)
    lane = iota((slots, 128), 1)
    stat = jnp.zeros((slots, 128), F32)
    for p, piece in enumerate(pieces(jnp.sum(sumsq, axis=1, keepdims=True))):
        stat = jnp.where(lane == p, piece, stat)
    out_ref[:, :, 2 * units :] = stat.astype(BF).reshape(slots // per, per, 128)


def activate(got_ref, out_ref):
    units = out_ref.shape[2]
    sums = jnp.sum(got_ref[...].astype(F32), axis=0)
    sumsq = jnp.sum(sums[:, 2 * units :], axis=1, keepdims=True)
    inverse = lax.rsqrt(sumsq / D + epsilon)
    gate = inverse * sums[:, :units]
    up = inverse * sums[:, units : 2 * units]
    active = (gate / (1.0 + jnp.exp(-gate)) * up).astype(BF)
    for c in range(out_ref.shape[0]):
        out_ref[c] = active


def down(got_ref, wd_ref, out_ref):
    n_ctx, per, units = got_ref.shape
    slots = n_ctx * per
    tiles = wd_ref.shape[2] // 128
    active = got_ref[...].reshape(slots, units)
    produced = dot(active, wd_ref[0]).astype(BF)
    stacked = jnp.concatenate([produced[:, 128 * k : 128 * (k + 1)] for k in range(tiles)], axis=0)
    size = slots * 8
    i, j = iota((size, tiles * slots), 0), iota((size, tiles * slots), 1)
    place = ((i // 8 == j % slots) & (i % 8 == j // slots)).astype(BF)
    out_ref[...] = dot(place, stacked).astype(BF).reshape(out_ref.shape)


def combine_rows(got_ref, combine_ref, hidden_ref, out_ref):
    rows, width = out_ref.shape
    n, span, _ = got_ref.shape
    mixed = dot(combine_ref[...], got_ref[...].reshape(n * span, 128), ((0,), (0,)))
    mixed = mixed[:64] + mixed[64:]
    for k in range(width // 128):
        at = slice(128 * k, 128 * (k + 1))
        out_ref[:, at] = (hidden_ref[:, at].astype(F32) + mixed[8 * k : 8 * k + rows]).astype(BF)


def on_device(
    queries,
    latent_cache,
    lengths,
    w_value,
    w_out,
    stream,
    norm_gain,
    expert_ids,
    gate_weights,
    w_gate,
    w_up,
    w_down,
):
    n_ctx = lax.axis_size("ctx")
    n_row = lax.axis_size("row")
    n_exp = lax.axis_size("exp")
    groups, heads, query_width = queries.shape
    block = latent_cache.shape[1]
    latent = w_value.shape[1]
    width = stream.shape[1]
    units = w_gate.shape[2]
    experts = n_row * n_exp
    slots = 2 * experts
    per = heads // n_ctx
    tiles = latent // 128
    span = groups * tiles * per + per

    route, combine = call(
        routing,
        (shape_of((slots * 8, 64), BF), shape_of((slots * 8, 128), BF)),
        (expert_ids, gate_weights),
        (slots * 8 * 64 * 100, slots * 8 * 400),
        in_specs=[pl.BlockSpec(memory_space=pltpu.SMEM)] * 2,
    )
    sent = pl.pallas_call(
        attend,
        out_shape=shape_of((n_ctx, span, 128), BF),
        in_specs=[
            pl.BlockSpec(memory_space=pltpu.HBM),
            pl.BlockSpec(memory_space=pltpu.HBM),
            pl.BlockSpec(memory_space=pltpu.HBM),
        ],
        scratch_shapes=[
            pltpu.VMEM((groups, query_width, heads), BF),
            pltpu.VMEM((groups, query_width, block), BF),
            pltpu.SMEM((groups,), I32),
            pltpu.SemaphoreType.DMA((2, groups)),
            pltpu.SemaphoreType.DMA,
        ],
        cost_estimate=pl.CostEstimate(
            flops=2 * groups * heads * block * (query_width + latent),
            bytes_accessed=2 * groups * (block + heads) * query_width,
            transcendentals=groups * heads * block,
        ),
        compiler_params=pltpu.CompilerParams(vmem_limit_bytes=53 * MIB),
    )(lengths, jnp.swapaxes(queries, 1, 2), jnp.swapaxes(latent_cache, 1, 2))
    got = exchange(sent, "ctx")
    sent = call(merge, shape_of((n_exp, groups * tiles, 128), BF), (got,), (1 << 22, 1 << 20))
    got = exchange(sent, "exp")
    sent = call(
        project,
        shape_of((n_exp, 2 * groups, D // 2), BF),
        (got, w_value, w_out),
        (2 * 128 * 256 * D // 2, 2 * 128 * D * 2),
    )
    got = exchange(sent, "exp")
    sent = call(add_heads, shape_of((n_ctx, groups, width), BF), (got,), (1 << 20, 1 << 20))
    got = exchange(sent, "ctx")
    hidden, sent = call(
        dispatch,
        (shape_of((groups, width), BF), shape_of((experts, 16, 128), BF)),
        (got, stream, route),
        (1 << 23, 1 << 19),
        scratch_shapes=[pltpu.VMEM((64, 128), F32)],
    )
    got = exchange(sent, ("row", "exp"))
    sent = call(
        gate_up,
        shape_of((n_ctx, slots // n_ctx, 2 * units + 128), BF),
        (got, norm_gain.reshape(1, width), w_gate, w_up),
        (4 * slots * width * units, 4 * width * units),
    )
    got = exchange(sent, "ctx")
    sent = call(activate, shape_of((n_ctx, slots // n_ctx, units), BF), (got,), (1 << 20, 1 << 19))
    got = exchange(sent, "ctx")
    sent = call(
        down,
        shape_of((experts, 16, 128), BF),
        (got, w_down),
        (2 * slots * width * units, 2 * width * units),
    )
    got = exchange(sent, ("row", "exp"))
    return call(
        combine_rows, shape_of((groups, width), BF), (got, combine, hidden), (1 << 24, 1 << 18)
    )


def solution(mesh):
    placed = (
        P(("row", "exp"), None, None),
        P(("row", "exp"), "ctx", None),
        P(("row", "exp")),
        P(("ctx", "exp"), None, None),
        P(("ctx", "exp"), None),
        P(("row", "exp"), "ctx"),
        P("ctx"),
        P(("row", "exp"), None),
        P(("row", "exp"), None),
        P(("row", "exp"), "ctx", None),
        P(("row", "exp"), "ctx", None),
        P(("row", "exp"), None, "ctx"),
    )
    return jax.shard_map(
        on_device, mesh=mesh, in_specs=placed, out_specs=P(("row", "exp"), "ctx"), check_vma=False
    )
```

```python
import functools

import jax
import jax.numpy as jnp
from jax import lax
from jax.experimental import pallas as pl
from jax.experimental.pallas import tpu as pltpu
from jax.sharding import PartitionSpec as P

D = 7168
QK_HEAD = 192
BF = jnp.bfloat16
F32 = jnp.float32
I32 = jnp.int32
epsilon = 1e-06
DEAD = -1e30
MIB = 1024 * 1024


def exchange(x, axes):
    return lax.all_to_all(x, axes, split_axis=0, concat_axis=0, tiled=True)


def dot(a, b, dims=((1,), (0,))):
    return lax.dot_general(a, b, (dims, ((), ())), preferred_element_type=F32)


def iota(shape, dim):
    return lax.broadcasted_iota(I32, shape, dim)


def pieces(x):
    hi = x.astype(BF).astype(F32)
    mid = (x - hi).astype(BF).astype(F32)
    low = (x - hi - mid).astype(BF).astype(F32)
    return hi, mid, low


def call(kernel, out, args, cost, **kw):
    return pl.pallas_call(
        kernel,
        out_shape=out,
        cost_estimate=pl.CostEstimate(flops=cost[0], bytes_accessed=cost[1], transcendentals=0),
        compiler_params=pltpu.CompilerParams(vmem_limit_bytes=24 * MIB),
        **kw,
    )(*args)


def shape_of(shape, dtype):
    return jax.ShapeDtypeStruct(shape, dtype)


def attend(length_hbm, q_hbm, kv_hbm, out_ref, q_ref, kv_ref, length_ref, sem, length_sem):
    rows, _, heads = q_ref.shape
    block = kv_ref.shape[2]
    n_ctx, span, _ = out_ref.shape
    per = heads // n_ctx
    tiles = (span - per) // per // rows
    latent = tiles * 128
    copies = []
    for r in range(rows):
        pair = (
            pltpu.make_async_copy(q_hbm.at[r], q_ref.at[r], sem.at[0, r]),
            pltpu.make_async_copy(kv_hbm.at[r], kv_ref.at[r], sem.at[1, r]),
        )
        for copy in pair:
            copy.start()
        copies.append(pair)
    length_copy = pltpu.make_async_copy(length_hbm, length_ref, length_sem)
    length_copy.start()
    length_copy.wait()
    first = lax.axis_index("ctx") * block
    lane = iota((heads, 128), 1)
    stat = jnp.zeros((heads, 128), F32)
    for r in range(rows):
        for copy in copies[r]:
            copy.wait()
        scores = dot(q_ref[r], kv_ref[r], ((0,), (0,))) * QK_HEAD ** (-0.5)
        live = iota((heads, block), 1) < length_ref[r] - first
        scores = jnp.where(live, scores, DEAD)
        top = jnp.max(scores, axis=1, keepdims=True)
        weights = jnp.where(live, jnp.exp(scores - top), 0.0)
        total = jnp.sum(weights, axis=1, keepdims=True)
        safe = jnp.where(total > 0, total, 1.0)
        part = dot(weights.astype(BF), kv_ref[r, :latent, :], ((1,), (1,))) * (1.0 / safe)
        part = part.astype(BF)
        for p, piece in enumerate(pieces(top + jnp.log(safe))):
            stat = jnp.where(lane == 4 * r + p, piece, stat)
        for c in range(n_ctx):
            for t in range(tiles):
                at = (r * tiles + t) * per
                out_ref[c, at : at + per, :] = part[per * c : per * (c + 1), 128 * t : 128 * (t + 1)]
    stat = stat.astype(BF)
    for c in range(n_ctx):
        out_ref[c, span - per :, :] = stat[per * c : per * (c + 1)]


def merge(got_ref, out_ref):
    n_ctx, span, _ = got_ref.shape
    per = out_ref.shape[0]
    rows = 4
    tiles = (span - per) // per // rows
    stat = got_ref[:, span - per :, :].astype(F32)
    lane = iota(stat.shape, 2)
    merged = []
    for r in range(rows):
        mine = (lane >= 4 * r) & (lane < 4 * r + 3)
        lse = jnp.sum(jnp.where(mine, stat, 0.0), axis=2, keepdims=True)
        factor = jnp.exp(lse - jnp.max(lse, axis=0, keepdims=True))
        factor = factor * (1.0 / jnp.sum(factor, axis=0, keepdims=True))
        for t in range(tiles):
            at = (r * tiles + t) * per
            merged.append(jnp.sum(factor * got_ref[:, at : at + per, :].astype(F32), axis=0))
    merged = jnp.concatenate(merged, axis=0).astype(BF)
    size = rows * tiles * per
    i, j = iota((size, size), 0), iota((size, size), 1)
    n = rows * tiles
    swap = ((i // n == j % per) & (i % n == j // per)).astype(BF)
    out_ref[...] = dot(swap, merged).astype(BF).reshape(out_ref.shape)


def project(got_ref, wv_ref, wo_ref, out_ref):
    n_exp, n, _ = got_ref.shape
    rows = 4
    tiles = n // rows
    size = n_exp * n
    count = n_exp * rows
    i, j = iota((size, size), 0), iota((size, size), 1)
    t, b = i // count, i % count
    pick = (j == (b // rows) * n + (b % rows) * tiles + t).astype(BF)
    latents = dot(pick, got_ref[...].reshape(size, 128)).astype(BF)
    values = jnp.zeros((count, wv_ref.shape[2]), F32)
    for t in range(tiles):
        values += dot(latents[count * t : count * (t + 1)], wv_ref[0, 128 * t : 128 * (t + 1), :])
    values = values.astype(BF)
    i, j = iota((2 * count, count), 0), iota((2 * count, count), 1)
    double = (j == (i // 8) * rows + i % rows).astype(BF)
    doubled = dot(double, values)
    upper = (iota(doubled.shape, 0) // rows) % 2
    lhs = jnp.concatenate(
        [jnp.where(upper == 0, doubled, 0.0), jnp.where(upper == 1, doubled, 0.0)], axis=1
    ).astype(BF)
    half = wo_ref.shape[1] // 2
    step = 512
    for at in range(0, half, step):
        rhs = jnp.concatenate([wo_ref[:, at : at + step], wo_ref[:, half + at : half + at + step]], axis=0)
        out_ref[:, :, at : at + step] = dot(lhs, rhs).astype(BF).reshape(n_exp, 8, step)


def add_heads(got_ref, out_ref):
    n_ctx, rows, width = out_ref.shape
    per = n_ctx // 2
    for q in range(per):
        total = jnp.sum(got_ref[:, :, width * q : width * (q + 1)].astype(F32), axis=0)
        out_ref[q] = total[:rows].astype(BF)
        out_ref[per + q] = total[rows:].astype(BF)


def dispatch(got_ref, stream_ref, route_ref, gain_ref, later_ref, hidden_ref, out_ref, scratch):
    del gain_ref, later_ref
    rows, width = stream_ref.shape
    hidden = (stream_ref[...].astype(F32) + jnp.sum(got_ref[...].astype(F32), axis=0)).astype(BF)
    hidden_ref[...] = hidden
    wide = hidden.astype(F32)
    scratch[...] = jnp.zeros_like(scratch)
    for k in range(width // 128):
        scratch[8 * k : 8 * k + rows, :] = wide[:, 128 * k : 128 * (k + 1)]
    out_ref[...] = dot(route_ref[...], scratch[...].astype(BF)).astype(BF).reshape(out_ref.shape)


def routing(ids_ref, weights_ref, route_ref, combine_ref):
    size = route_ref.shape[0]
    rows, picks = ids_ref.shape
    i, j = iota((size, 64), 0), iota((size, 64), 1)
    expert, slot = i // 16, (i // 8) % 2
    same = (i % 8) == (j // 8)
    count = jnp.zeros((size, 64), I32)
    route = jnp.zeros((size, 64), F32)
    combine = jnp.zeros((size, 64), F32)
    for b in range(rows):
        weight = jnp.zeros((size, 64), F32)
        named = jnp.zeros((size, 64), I32)
        for k in range(picks):
            hit = expert == ids_ref[b, k]
            weight = jnp.where(hit, weights_ref[b, k], weight)
            named = jnp.where(hit, 1, named)
        mine = (named == 1) & (count == slot) & same & (j % 8 == b)
        route = jnp.where(mine, 1.0, route)
        combine = jnp.where(mine, weight, combine)
        count = count + named
    route_ref[...] = route.astype(BF)
    hi = combine.astype(BF)
    low = (combine - hi.astype(F32)).astype(BF)
    combine_ref[...] = jnp.concatenate([hi, low], axis=1)


def gate_up(got_ref, gain_ref, wg_ref, wu_ref, out_ref):
    n, span, _ = got_ref.shape
    slots = n * span // 8
    tiles = wg_ref.shape[1] // 128
    i, j = iota((tiles * slots, n * span), 0), iota((tiles * slots, n * span), 1)
    pick = ((j // 8 == i % slots) & (j % 8 == i // slots)).astype(BF)
    rows = dot(pick, got_ref[...].reshape(n * span, 128))
    sumsq = jnp.zeros((slots, 128), F32)
    scaled = []
    for k in range(tiles):
        part = rows[slots * k : slots * (k + 1)]
        sumsq += part * part
        scaled.append((part * gain_ref[:, 128 * k : 128 * (k + 1)]).astype(BF))
    scaled = jnp.concatenate(scaled, axis=1)
    units = wg_ref.shape[2]
    step = 512
    per = out_ref.shape[1]
    for w_ref, base in ((wg_ref, 0), (wu_ref, units)):
        for at in range(0, units, step):
            part = dot(scaled, w_ref[0, :, at : at + step]).astype(BF)
            out_ref[:, :, base + at : base + at + step] = part.reshape(slots // per, per, step)
    lane = iota((slots, 128), 1)
    stat = jnp.zeros((slots, 128), F32)
    for p, piece in enumerate(pieces(jnp.sum(sumsq, axis=1, keepdims=True))):
        stat = jnp.where(lane == p, piece, stat)
    out_ref[:, :, 2 * units :] = stat.astype(BF).reshape(slots // per, per, 128)


def activate(got_ref, out_ref):
    units = out_ref.shape[2]
    sums = jnp.sum(got_ref[...].astype(F32), axis=0)
    sumsq = jnp.sum(sums[:, 2 * units :], axis=1, keepdims=True)
    inverse = lax.rsqrt(sumsq / D + epsilon)
    gate = inverse * sums[:, :units]
    up = inverse * sums[:, units : 2 * units]
    active = (gate / (1.0 + jnp.exp(-gate)) * up).astype(BF)
    for c in range(out_ref.shape[0]):
        out_ref[c] = active


def down(got_ref, wd_ref, out_ref):
    n_ctx, per, units = got_ref.shape
    slots = n_ctx * per
    tiles = wd_ref.shape[2] // 128
    active = got_ref[...].reshape(slots, units)
    produced = dot(active, wd_ref[0]).astype(BF)
    stacked = jnp.concatenate([produced[:, 128 * k : 128 * (k + 1)] for k in range(tiles)], axis=0)
    size = slots * 8
    i, j = iota((size, tiles * slots), 0), iota((size, tiles * slots), 1)
    place = ((i // 8 == j % slots) & (i % 8 == j // slots)).astype(BF)
    out_ref[...] = dot(place, stacked).astype(BF).reshape(out_ref.shape)


def combine_rows(got_ref, combine_ref, hidden_ref, out_ref):
    rows, width = out_ref.shape
    n, span, _ = got_ref.shape
    mixed = dot(combine_ref[...], got_ref[...].reshape(n * span, 128), ((0,), (0,)))
    mixed = mixed[:64] + mixed[64:]
    for k in range(width // 128):
        at = slice(128 * k, 128 * (k + 1))
        out_ref[:, at] = (hidden_ref[:, at].astype(F32) + mixed[8 * k : 8 * k + rows]).astype(BF)


def on_device(
    queries,
    latent_cache,
    lengths,
    w_value,
    w_out,
    stream,
    norm_gain,
    expert_ids,
    gate_weights,
    w_gate,
    w_up,
    w_down,
):
    n_ctx = lax.axis_size("ctx")
    n_row = lax.axis_size("row")
    n_exp = lax.axis_size("exp")
    groups, heads, query_width = queries.shape
    block = latent_cache.shape[1]
    latent = w_value.shape[1]
    width = stream.shape[1]
    units = w_gate.shape[2]
    experts = n_row * n_exp
    slots = 2 * experts
    per = heads // n_ctx
    tiles = latent // 128
    span = groups * tiles * per + per

    vmem = pl.BlockSpec(memory_space=pltpu.VMEM)
    anywhere = pl.BlockSpec(memory_space=pl.ANY)
    gain = norm_gain.reshape(1, width)
    route, combine = call(
        routing,
        (shape_of((slots * 8, 64), BF), shape_of((slots * 8, 128), BF)),
        (expert_ids, gate_weights),
        (slots * 8 * 64 * 100, slots * 8 * 400),
        in_specs=[pl.BlockSpec(memory_space=pltpu.SMEM)] * 2,
    )
    sent = pl.pallas_call(
        attend,
        out_shape=shape_of((n_ctx, span, 128), BF),
        in_specs=[
            pl.BlockSpec(memory_space=pltpu.HBM),
            pl.BlockSpec(memory_space=pltpu.HBM),
            pl.BlockSpec(memory_space=pltpu.HBM),
        ],
        scratch_shapes=[
            pltpu.VMEM((groups, query_width, heads), BF),
            pltpu.VMEM((groups, query_width, block), BF),
            pltpu.SMEM((groups,), I32),
            pltpu.SemaphoreType.DMA((2, groups)),
            pltpu.SemaphoreType.DMA,
        ],
        cost_estimate=pl.CostEstimate(
            flops=2 * groups * heads * block * (query_width + latent),
            bytes_accessed=2 * groups * (block + heads) * query_width,
            transcendentals=groups * heads * block,
        ),
        compiler_params=pltpu.CompilerParams(vmem_limit_bytes=53 * MIB),
    )(lengths, jnp.swapaxes(queries, 1, 2), jnp.swapaxes(latent_cache, 1, 2))
    got = exchange(sent, "ctx")
    sent = call(merge, shape_of((n_exp, groups * tiles, 128), BF), (got,), (1 << 22, 1 << 20))
    got = exchange(sent, "exp")
    sent = call(
        project,
        shape_of((n_exp, 2 * groups, D // 2), BF),
        (got, w_value, w_out),
        (2 * 128 * 256 * D // 2, 2 * 128 * D * 2),
    )
    got = exchange(sent, "exp")
    sent = call(add_heads, shape_of((n_ctx, groups, width), BF), (got,), (1 << 20, 1 << 20))
    got = exchange(sent, "ctx")
    hidden, sent = call(
        dispatch,
        (shape_of((groups, width), BF), shape_of((experts, 16, 128), BF)),
        (got, stream, route, gain, w_up),
        (1 << 23, 1 << 19),
        in_specs=[vmem] * 3 + [anywhere] * 2,
        scratch_shapes=[pltpu.VMEM((64, 128), F32)],
    )
    got = exchange(sent, ("row", "exp"))
    sent = call(
        gate_up,
        shape_of((n_ctx, slots // n_ctx, 2 * units + 128), BF),
        (got, gain, w_gate, w_up),
        (4 * slots * width * units, 4 * width * units),
    )
    got = exchange(sent, "ctx")
    sent = call(activate, shape_of((n_ctx, slots // n_ctx, units), BF), (got,), (1 << 20, 1 << 19))
    got = exchange(sent, "ctx")
    sent = call(
        down,
        shape_of((experts, 16, 128), BF),
        (got, w_down),
        (2 * slots * width * units, 2 * width * units),
    )
    got = exchange(sent, ("row", "exp"))
    return call(
        combine_rows, shape_of((groups, width), BF), (got, combine, hidden), (1 << 24, 1 << 18)
    )


def solution(mesh):
    placed = (
        P(("row", "exp"), None, None),
        P(("row", "exp"), "ctx", None),
        P(("row", "exp")),
        P(("ctx", "exp"), None, None),
        P(("ctx", "exp"), None),
        P(("row", "exp"), "ctx"),
        P("ctx"),
        P(("row", "exp"), None),
        P(("row", "exp"), None),
        P(("row", "exp"), "ctx", None),
        P(("row", "exp"), "ctx", None),
        P(("row", "exp"), None, "ctx"),
    )
    return jax.shard_map(
        on_device, mesh=mesh, in_specs=placed, out_specs=P(("row", "exp"), "ctx"), check_vma=False
    )
```

```python
import functools

import jax
import jax.numpy as jnp
from jax import lax
from jax.experimental import pallas as pl
from jax.experimental.pallas import tpu as pltpu
from jax.sharding import PartitionSpec as P

D = 7168
QK_HEAD = 192
BF = jnp.bfloat16
F32 = jnp.float32
I32 = jnp.int32
epsilon = 1e-06
DEAD = -1e30
MIB = 1024 * 1024


def exchange(x, axes):
    return lax.all_to_all(x, axes, split_axis=0, concat_axis=0, tiled=True)


def dot(a, b, dims=((1,), (0,))):
    return lax.dot_general(a, b, (dims, ((), ())), preferred_element_type=F32)


def iota(shape, dim):
    return lax.broadcasted_iota(I32, shape, dim)


def pieces(x):
    hi = x.astype(BF).astype(F32)
    mid = (x - hi).astype(BF).astype(F32)
    low = (x - hi - mid).astype(BF).astype(F32)
    return hi, mid, low


def call(kernel, out, args, cost, **kw):
    return pl.pallas_call(
        kernel,
        out_shape=out,
        cost_estimate=pl.CostEstimate(flops=cost[0], bytes_accessed=cost[1], transcendentals=0),
        compiler_params=pltpu.CompilerParams(vmem_limit_bytes=24 * MIB),
        **kw,
    )(*args)


def shape_of(shape, dtype):
    return jax.ShapeDtypeStruct(shape, dtype)


def attend(length_hbm, q_hbm, kv_hbm, out_ref, q_ref, kv_ref, length_ref, sem, length_sem):
    rows, _, heads = q_ref.shape
    block = kv_ref.shape[2]
    n_ctx, span, _ = out_ref.shape
    per = heads // n_ctx
    tiles = (span - per) // per // rows
    latent = tiles * 128
    copies = []
    for r in range(rows):
        pair = (
            pltpu.make_async_copy(q_hbm.at[r], q_ref.at[r], sem.at[0, r]),
            pltpu.make_async_copy(kv_hbm.at[r], kv_ref.at[r], sem.at[1, r]),
        )
        for copy in pair:
            copy.start()
        copies.append(pair)
    length_copy = pltpu.make_async_copy(length_hbm, length_ref, length_sem)
    length_copy.start()
    length_copy.wait()
    first = lax.axis_index("ctx") * block
    lane = iota((heads, 128), 1)
    stat = jnp.zeros((heads, 128), F32)
    for r in range(rows):
        for copy in copies[r]:
            copy.wait()
        scores = dot(q_ref[r], kv_ref[r], ((0,), (0,))) * QK_HEAD ** (-0.5)
        live = iota((heads, block), 1) < length_ref[r] - first
        scores = jnp.where(live, scores, DEAD)
        top = jnp.max(scores, axis=1, keepdims=True)
        weights = jnp.where(live, jnp.exp(scores - top), 0.0)
        total = jnp.sum(weights, axis=1, keepdims=True)
        safe = jnp.where(total > 0, total, 1.0)
        part = dot(weights.astype(BF), kv_ref[r, :latent, :], ((1,), (1,))) * (1.0 / safe)
        part = part.astype(BF)
        for p, piece in enumerate(pieces(top + jnp.log(safe))):
            stat = jnp.where(lane == 4 * r + p, piece, stat)
        for c in range(n_ctx):
            for t in range(tiles):
                at = (r * tiles + t) * per
                out_ref[c, at : at + per, :] = part[per * c : per * (c + 1), 128 * t : 128 * (t + 1)]
    stat = stat.astype(BF)
    for c in range(n_ctx):
        out_ref[c, span - per :, :] = stat[per * c : per * (c + 1)]


def merge(got_ref, out_ref, scratch):
    n_ctx, span, _ = got_ref.shape
    per = out_ref.shape[0]
    rows = 4
    tiles = (span - per) // per // rows
    stat = got_ref[:, span - per :, :].astype(F32)
    lane = iota(stat.shape, 2)
    n = rows * tiles
    for r in range(rows):
        mine = (lane >= 4 * r) & (lane < 4 * r + 3)
        lse = jnp.sum(jnp.where(mine, stat, 0.0), axis=2, keepdims=True)
        factor = jnp.exp(lse - jnp.max(lse, axis=0, keepdims=True))
        factor = factor * (1.0 / jnp.sum(factor, axis=0, keepdims=True))
        for t in range(tiles):
            at = r * tiles + t
            part = got_ref[:, at * per : (at + 1) * per, :].astype(F32)
            scratch[pl.ds(at, per, stride=n), :] = jnp.sum(factor * part, axis=0)
    out_ref[...] = scratch[...].astype(BF).reshape(out_ref.shape)


def project(got_ref, wv_ref, wo_ref, out_ref, got_wide, values_wide, upper, lower):
    n_exp, n, _ = got_ref.shape
    rows = 4
    tiles = n // rows
    size = n_exp * n
    count = n_exp * rows
    got_wide[...] = got_ref[...].astype(F32).reshape(size, 128)
    values = jnp.zeros((count, wv_ref.shape[2]), F32)
    for t in range(tiles):
        latents = got_wide[pl.ds(t, count, stride=tiles), :].astype(BF)
        values += dot(latents, wv_ref[0, 128 * t : 128 * (t + 1), :])
    values_wide[...] = values
    upper[...] = jnp.zeros_like(upper)
    lower[...] = jnp.zeros_like(lower)
    for b in range(rows):
        line = values_wide[pl.ds(b, n_exp, stride=rows), :]
        upper[pl.ds(b, n_exp, stride=8), :] = line
        lower[pl.ds(rows + b, n_exp, stride=8), :] = line
    lhs = jnp.concatenate([upper[...], lower[...]], axis=1).astype(BF)
    half = wo_ref.shape[1] // 2
    step = 512
    for at in range(0, half, step):
        rhs = jnp.concatenate([wo_ref[:, at : at + step], wo_ref[:, half + at : half + at + step]], axis=0)
        out_ref[:, :, at : at + step] = dot(lhs, rhs).astype(BF).reshape(n_exp, 8, step)


def add_heads(got_ref, out_ref):
    n_ctx, rows, width = out_ref.shape
    per = n_ctx // 2
    for q in range(per):
        total = jnp.sum(got_ref[:, :, width * q : width * (q + 1)].astype(F32), axis=0)
        out_ref[q] = total[:rows].astype(BF)
        out_ref[per + q] = total[rows:].astype(BF)


def dispatch(got_ref, stream_ref, route_ref, gain_ref, later_ref, hidden_ref, out_ref, scratch):
    del gain_ref, later_ref
    rows, width = stream_ref.shape
    hidden = (stream_ref[...].astype(F32) + jnp.sum(got_ref[...].astype(F32), axis=0)).astype(BF)
    hidden_ref[...] = hidden
    wide = hidden.astype(F32)
    scratch[...] = jnp.zeros_like(scratch)
    for k in range(width // 128):
        scratch[8 * k : 8 * k + rows, :] = wide[:, 128 * k : 128 * (k + 1)]
    out_ref[...] = dot(route_ref[...], scratch[...].astype(BF)).astype(BF).reshape(out_ref.shape)


def routing(ids_ref, weights_ref, route_ref, combine_ref):
    size = route_ref.shape[0]
    rows, picks = ids_ref.shape
    i, j = iota((size, 64), 0), iota((size, 64), 1)
    expert, slot = i // 16, (i // 8) % 2
    same = (i % 8) == (j // 8)
    count = jnp.zeros((size, 64), I32)
    route = jnp.zeros((size, 64), F32)
    combine = jnp.zeros((size, 64), F32)
    for b in range(rows):
        weight = jnp.zeros((size, 64), F32)
        named = jnp.zeros((size, 64), I32)
        for k in range(picks):
            hit = expert == ids_ref[b, k]
            weight = jnp.where(hit, weights_ref[b, k], weight)
            named = jnp.where(hit, 1, named)
        mine = (named == 1) & (count == slot) & same & (j % 8 == b)
        route = jnp.where(mine, 1.0, route)
        combine = jnp.where(mine, weight, combine)
        count = count + named
    route_ref[...] = route.astype(BF)
    hi = combine.astype(BF)
    low = (combine - hi.astype(F32)).astype(BF)
    combine_ref[...] = jnp.concatenate([hi, low], axis=1)


def gate_up(got_ref, gain_ref, wg_ref, wu_ref, out_ref, scratch):
    n, span, _ = got_ref.shape
    slots = n * span // 8
    tiles = wg_ref.shape[1] // 128
    scratch[...] = got_ref[...].astype(F32).reshape(n * span, 128)
    sumsq = jnp.zeros((slots, 128), F32)
    scaled = []
    for k in range(tiles):
        part = scratch[pl.ds(k, slots, stride=8), :]
        sumsq += part * part
        scaled.append((part * gain_ref[:, 128 * k : 128 * (k + 1)]).astype(BF))
    scaled = jnp.concatenate(scaled, axis=1)
    units = wg_ref.shape[2]
    step = 512
    per = out_ref.shape[1]
    for w_ref, base in ((wg_ref, 0), (wu_ref, units)):
        for at in range(0, units, step):
            part = dot(scaled, w_ref[0, :, at : at + step]).astype(BF)
            out_ref[:, :, base + at : base + at + step] = part.reshape(slots // per, per, step)
    lane = iota((slots, 128), 1)
    stat = jnp.zeros((slots, 128), F32)
    for p, piece in enumerate(pieces(jnp.sum(sumsq, axis=1, keepdims=True))):
        stat = jnp.where(lane == p, piece, stat)
    out_ref[:, :, 2 * units :] = stat.astype(BF).reshape(slots // per, per, 128)


def activate(got_ref, out_ref):
    units = out_ref.shape[2]
    sums = jnp.sum(got_ref[...].astype(F32), axis=0)
    sumsq = jnp.sum(sums[:, 2 * units :], axis=1, keepdims=True)
    inverse = lax.rsqrt(sumsq / D + epsilon)
    gate = inverse * sums[:, :units]
    up = inverse * sums[:, units : 2 * units]
    active = (gate / (1.0 + jnp.exp(-gate)) * up).astype(BF)
    for c in range(out_ref.shape[0]):
        out_ref[c] = active


def down(got_ref, wd_ref, out_ref, scratch):
    n_ctx, per, units = got_ref.shape
    slots = n_ctx * per
    tiles = wd_ref.shape[2] // 128
    active = got_ref[...].reshape(slots, units)
    produced = dot(active, wd_ref[0])
    for k in range(tiles):
        scratch[pl.ds(k, slots, stride=8), :] = produced[:, 128 * k : 128 * (k + 1)]
    scratch[pl.ds(tiles, slots, stride=8), :] = jnp.zeros((slots, 128), F32)
    out_ref[...] = scratch[...].astype(BF).reshape(out_ref.shape)


def combine_rows(got_ref, combine_ref, hidden_ref, out_ref):
    rows, width = out_ref.shape
    n, span, _ = got_ref.shape
    mixed = dot(combine_ref[...], got_ref[...].reshape(n * span, 128), ((0,), (0,)))
    mixed = mixed[:64] + mixed[64:]
    for k in range(width // 128):
        at = slice(128 * k, 128 * (k + 1))
        out_ref[:, at] = (hidden_ref[:, at].astype(F32) + mixed[8 * k : 8 * k + rows]).astype(BF)


def on_device(
    queries,
    latent_cache,
    lengths,
    w_value,
    w_out,
    stream,
    norm_gain,
    expert_ids,
    gate_weights,
    w_gate,
    w_up,
    w_down,
):
    n_ctx = lax.axis_size("ctx")
    n_row = lax.axis_size("row")
    n_exp = lax.axis_size("exp")
    groups, heads, query_width = queries.shape
    block = latent_cache.shape[1]
    latent = w_value.shape[1]
    width = stream.shape[1]
    units = w_gate.shape[2]
    experts = n_row * n_exp
    slots = 2 * experts
    per = heads // n_ctx
    tiles = latent // 128
    span = groups * tiles * per + per

    vmem = pl.BlockSpec(memory_space=pltpu.VMEM)
    anywhere = pl.BlockSpec(memory_space=pl.ANY)
    gain = norm_gain.reshape(1, width)
    route, combine = call(
        routing,
        (shape_of((slots * 8, 64), BF), shape_of((slots * 8, 128), BF)),
        (expert_ids, gate_weights),
        (slots * 8 * 64 * 100, slots * 8 * 400),
        in_specs=[pl.BlockSpec(memory_space=pltpu.SMEM)] * 2,
    )
    sent = pl.pallas_call(
        attend,
        out_shape=shape_of((n_ctx, span, 128), BF),
        in_specs=[
            pl.BlockSpec(memory_space=pltpu.HBM),
            pl.BlockSpec(memory_space=pltpu.HBM),
            pl.BlockSpec(memory_space=pltpu.HBM),
        ],
        scratch_shapes=[
            pltpu.VMEM((groups, query_width, heads), BF),
            pltpu.VMEM((groups, query_width, block), BF),
            pltpu.SMEM((groups,), I32),
            pltpu.SemaphoreType.DMA((2, groups)),
            pltpu.SemaphoreType.DMA,
        ],
        cost_estimate=pl.CostEstimate(
            flops=2 * groups * heads * block * (query_width + latent),
            bytes_accessed=2 * groups * (block + heads) * query_width,
            transcendentals=groups * heads * block,
        ),
        compiler_params=pltpu.CompilerParams(vmem_limit_bytes=53 * MIB),
    )(lengths, jnp.swapaxes(queries, 1, 2), jnp.swapaxes(latent_cache, 1, 2))
    got = exchange(sent, "ctx")
    sent = call(
        merge,
        shape_of((n_exp, groups * tiles, 128), BF),
        (got,),
        (1 << 22, 1 << 20),
        scratch_shapes=[pltpu.VMEM((n_exp * groups * tiles, 128), F32)],
    )
    got = exchange(sent, "exp")
    sent = call(
        project,
        shape_of((n_exp, 2 * groups, D // 2), BF),
        (got, w_value, w_out),
        (2 * 128 * 256 * D // 2, 2 * 128 * D * 2),
        scratch_shapes=[
            pltpu.VMEM((n_exp * groups * tiles, 128), F32),
            pltpu.VMEM((n_exp * groups, 128), F32),
            pltpu.VMEM((2 * n_exp * groups, 128), F32),
            pltpu.VMEM((2 * n_exp * groups, 128), F32),
        ],
    )
    got = exchange(sent, "exp")
    sent = call(add_heads, shape_of((n_ctx, groups, width), BF), (got,), (1 << 20, 1 << 20))
    got = exchange(sent, "ctx")
    hidden, sent = call(
        dispatch,
        (shape_of((groups, width), BF), shape_of((experts, 16, 128), BF)),
        (got, stream, route, gain, w_up),
        (1 << 23, 1 << 19),
        in_specs=[vmem] * 3 + [anywhere] * 2,
        scratch_shapes=[pltpu.VMEM((64, 128), F32)],
    )
    got = exchange(sent, ("row", "exp"))
    sent = call(
        gate_up,
        shape_of((n_ctx, slots // n_ctx, 2 * units + 128), BF),
        (got, gain, w_gate, w_up),
        (4 * slots * width * units, 4 * width * units),
        scratch_shapes=[pltpu.VMEM((slots * 8, 128), F32)],
    )
    got = exchange(sent, "ctx")
    sent = call(activate, shape_of((n_ctx, slots // n_ctx, units), BF), (got,), (1 << 20, 1 << 19))
    got = exchange(sent, "ctx")
    sent = call(
        down,
        shape_of((experts, 16, 128), BF),
        (got, w_down),
        (2 * slots * width * units, 2 * width * units),
        scratch_shapes=[pltpu.VMEM((slots * 8, 128), F32)],
    )
    got = exchange(sent, ("row", "exp"))
    return call(
        combine_rows, shape_of((groups, width), BF), (got, combine, hidden), (1 << 24, 1 << 18)
    )


def solution(mesh):
    placed = (
        P(("row", "exp"), None, None),
        P(("row", "exp"), "ctx", None),
        P(("row", "exp")),
        P(("ctx", "exp"), None, None),
        P(("ctx", "exp"), None),
        P(("row", "exp"), "ctx"),
        P("ctx"),
        P(("row", "exp"), None),
        P(("row", "exp"), None),
        P(("row", "exp"), "ctx", None),
        P(("row", "exp"), "ctx", None),
        P(("row", "exp"), None, "ctx"),
    )
    return jax.shard_map(
        on_device, mesh=mesh, in_specs=placed, out_specs=P(("row", "exp"), "ctx"), check_vma=False
    )
```

```python
import functools

import jax
import jax.numpy as jnp
from jax import lax
from jax.experimental import pallas as pl
from jax.experimental.pallas import tpu as pltpu
from jax.sharding import PartitionSpec as P

D = 7168
QK_HEAD = 192
BF = jnp.bfloat16
F32 = jnp.float32
I32 = jnp.int32
epsilon = 1e-06
DEAD = -1e30
MIB = 1024 * 1024


def exchange(x, axes):
    return lax.all_to_all(x, axes, split_axis=0, concat_axis=0, tiled=True)


def dot(a, b, dims=((1,), (0,))):
    return lax.dot_general(a, b, (dims, ((), ())), preferred_element_type=F32)


def iota(shape, dim):
    return lax.broadcasted_iota(I32, shape, dim)


def pieces(x):
    hi = x.astype(BF).astype(F32)
    mid = (x - hi).astype(BF).astype(F32)
    low = (x - hi - mid).astype(BF).astype(F32)
    return hi, mid, low


def call(kernel, out, args, cost, **kw):
    return pl.pallas_call(
        kernel,
        out_shape=out,
        cost_estimate=pl.CostEstimate(flops=cost[0], bytes_accessed=cost[1], transcendentals=0),
        compiler_params=pltpu.CompilerParams(vmem_limit_bytes=24 * MIB),
        **kw,
    )(*args)


def shape_of(shape, dtype):
    return jax.ShapeDtypeStruct(shape, dtype)


def attend(length_hbm, q_hbm, kv_hbm, out_ref, q_ref, kv_ref, length_ref, sem, length_sem):
    rows, _, heads = q_ref.shape
    block = kv_ref.shape[2]
    n_ctx, span, _ = out_ref.shape
    per = heads // n_ctx
    tiles = (span - per) // per // rows
    latent = tiles * 128
    copies = []
    for r in range(rows):
        pair = (
            pltpu.make_async_copy(q_hbm.at[r], q_ref.at[r], sem.at[0, r]),
            pltpu.make_async_copy(kv_hbm.at[r], kv_ref.at[r], sem.at[1, r]),
        )
        for copy in pair:
            copy.start()
        copies.append(pair)
    length_copy = pltpu.make_async_copy(length_hbm, length_ref, length_sem)
    length_copy.start()
    length_copy.wait()
    first = lax.axis_index("ctx") * block
    lane = iota((heads, 128), 1)
    stat = jnp.zeros((heads, 128), F32)

    def products(r):
        for copy in copies[r]:
            copy.wait()
        return dot(q_ref[r], kv_ref[r], ((0,), (0,))) * QK_HEAD ** (-0.5)

    following = products(0)
    for r in range(rows):
        scores = following
        if r + 1 < rows:
            following = products(r + 1)
        live = iota((heads, block), 1) < length_ref[r] - first
        scores = jnp.where(live, scores, DEAD)
        top = jnp.max(scores, axis=1, keepdims=True)
        weights = jnp.where(live, jnp.exp(scores - top), 0.0)
        total = jnp.sum(weights, axis=1, keepdims=True)
        safe = jnp.where(total > 0, total, 1.0)
        part = dot(weights.astype(BF), kv_ref[r, :latent, :], ((1,), (1,))) * (1.0 / safe)
        part = part.astype(BF)
        for p, piece in enumerate(pieces(top + jnp.log(safe))):
            stat = jnp.where(lane == 4 * r + p, piece, stat)
        for c in range(n_ctx):
            for t in range(tiles):
                at = (r * tiles + t) * per
                out_ref[c, at : at + per, :] = part[per * c : per * (c + 1), 128 * t : 128 * (t + 1)]
    stat = stat.astype(BF)
    for c in range(n_ctx):
        out_ref[c, span - per :, :] = stat[per * c : per * (c + 1)]


def merge(got_ref, out_ref, scratch):
    n_ctx, span, _ = got_ref.shape
    per = out_ref.shape[0]
    rows = 4
    tiles = (span - per) // per // rows
    stat = got_ref[:, span - per :, :].astype(F32)
    lane = iota(stat.shape, 2)
    n = rows * tiles
    for r in range(rows):
        mine = (lane >= 4 * r) & (lane < 4 * r + 3)
        lse = jnp.sum(jnp.where(mine, stat, 0.0), axis=2, keepdims=True)
        factor = jnp.exp(lse - jnp.max(lse, axis=0, keepdims=True))
        factor = factor * (1.0 / jnp.sum(factor, axis=0, keepdims=True))
        for t in range(tiles):
            at = r * tiles + t
            part = got_ref[:, at * per : (at + 1) * per, :].astype(F32)
            scratch[pl.ds(at, per, stride=n), :] = jnp.sum(factor * part, axis=0)
    out_ref[...] = scratch[...].astype(BF).reshape(out_ref.shape)


def project(got_ref, wv_ref, wo_ref, out_ref, got_wide, values_wide, upper, lower):
    n_exp, n, _ = got_ref.shape
    rows = 4
    tiles = n // rows
    size = n_exp * n
    count = n_exp * rows
    got_wide[...] = got_ref[...].astype(F32).reshape(size, 128)
    values = jnp.zeros((count, wv_ref.shape[2]), F32)
    for t in range(tiles):
        latents = got_wide[pl.ds(t, count, stride=tiles), :].astype(BF)
        values += dot(latents, wv_ref[0, 128 * t : 128 * (t + 1), :])
    values_wide[...] = values
    upper[...] = jnp.zeros_like(upper)
    lower[...] = jnp.zeros_like(lower)
    for b in range(rows):
        line = values_wide[pl.ds(b, n_exp, stride=rows), :]
        upper[pl.ds(b, n_exp, stride=8), :] = line
        lower[pl.ds(rows + b, n_exp, stride=8), :] = line
    lhs = jnp.concatenate([upper[...], lower[...]], axis=1).astype(BF)
    half = wo_ref.shape[1] // 2
    step = 512
    for at in range(0, half, step):
        rhs = jnp.concatenate([wo_ref[:, at : at + step], wo_ref[:, half + at : half + at + step]], axis=0)
        out_ref[:, :, at : at + step] = dot(lhs, rhs).astype(BF).reshape(n_exp, 8, step)


def add_heads(got_ref, out_ref):
    n_ctx, rows, width = out_ref.shape
    per = n_ctx // 2
    for q in range(per):
        total = jnp.sum(got_ref[:, :, width * q : width * (q + 1)].astype(F32), axis=0)
        out_ref[q] = total[:rows].astype(BF)
        out_ref[per + q] = total[rows:].astype(BF)


def dispatch(got_ref, stream_ref, route_ref, gain_ref, later_ref, hidden_ref, out_ref, scratch):
    del gain_ref, later_ref
    rows, width = stream_ref.shape
    hidden = (stream_ref[...].astype(F32) + jnp.sum(got_ref[...].astype(F32), axis=0)).astype(BF)
    hidden_ref[...] = hidden
    wide = hidden.astype(F32)
    scratch[...] = jnp.zeros_like(scratch)
    for k in range(width // 128):
        scratch[8 * k : 8 * k + rows, :] = wide[:, 128 * k : 128 * (k + 1)]
    out_ref[...] = dot(route_ref[...], scratch[...].astype(BF)).astype(BF).reshape(out_ref.shape)


def routing(ids_ref, weights_ref, route_ref, combine_ref):
    size = route_ref.shape[0]
    rows, picks = ids_ref.shape
    i, j = iota((size, 64), 0), iota((size, 64), 1)
    expert, slot = i // 16, (i // 8) % 2
    same = (i % 8) == (j // 8)
    count = jnp.zeros((size, 64), I32)
    route = jnp.zeros((size, 64), F32)
    combine = jnp.zeros((size, 64), F32)
    for b in range(rows):
        weight = jnp.zeros((size, 64), F32)
        named = jnp.zeros((size, 64), I32)
        for k in range(picks):
            hit = expert == ids_ref[b, k]
            weight = jnp.where(hit, weights_ref[b, k], weight)
            named = jnp.where(hit, 1, named)
        mine = (named == 1) & (count == slot) & same & (j % 8 == b)
        route = jnp.where(mine, 1.0, route)
        combine = jnp.where(mine, weight, combine)
        count = count + named
    route_ref[...] = route.astype(BF)
    hi = combine.astype(BF)
    low = (combine - hi.astype(F32)).astype(BF)
    combine_ref[...] = jnp.concatenate([hi, low], axis=1)


def gate_up(got_ref, gain_ref, wg_ref, wu_ref, out_ref, scratch):
    n, span, _ = got_ref.shape
    slots = n * span // 8
    tiles = wg_ref.shape[1] // 128
    scratch[...] = got_ref[...].astype(F32).reshape(n * span, 128)
    sumsq = jnp.zeros((slots, 128), F32)
    scaled = []
    for k in range(tiles):
        part = scratch[pl.ds(k, slots, stride=8), :]
        sumsq += part * part
        scaled.append((part * gain_ref[:, 128 * k : 128 * (k + 1)]).astype(BF))
    scaled = jnp.concatenate(scaled, axis=1)
    units = wg_ref.shape[2]
    step = 512
    per = out_ref.shape[1]
    for w_ref, base in ((wg_ref, 0), (wu_ref, units)):
        for at in range(0, units, step):
            part = dot(scaled, w_ref[0, :, at : at + step]).astype(BF)
            out_ref[:, :, base + at : base + at + step] = part.reshape(slots // per, per, step)
    lane = iota((slots, 128), 1)
    stat = jnp.zeros((slots, 128), F32)
    for p, piece in enumerate(pieces(jnp.sum(sumsq, axis=1, keepdims=True))):
        stat = jnp.where(lane == p, piece, stat)
    out_ref[:, :, 2 * units :] = stat.astype(BF).reshape(slots // per, per, 128)


def activate(got_ref, out_ref):
    units = out_ref.shape[2]
    sums = jnp.sum(got_ref[...].astype(F32), axis=0)
    sumsq = jnp.sum(sums[:, 2 * units :], axis=1, keepdims=True)
    inverse = lax.rsqrt(sumsq / D + epsilon)
    gate = inverse * sums[:, :units]
    up = inverse * sums[:, units : 2 * units]
    active = (gate / (1.0 + jnp.exp(-gate)) * up).astype(BF)
    for c in range(out_ref.shape[0]):
        out_ref[c] = active


def down(got_ref, wd_ref, out_ref, scratch):
    n_ctx, per, units = got_ref.shape
    slots = n_ctx * per
    tiles = wd_ref.shape[2] // 128
    active = got_ref[...].reshape(slots, units)
    produced = dot(active, wd_ref[0])
    for k in range(tiles):
        scratch[pl.ds(k, slots, stride=8), :] = produced[:, 128 * k : 128 * (k + 1)]
    scratch[pl.ds(tiles, slots, stride=8), :] = jnp.zeros((slots, 128), F32)
    out_ref[...] = scratch[...].astype(BF).reshape(out_ref.shape)


def combine_rows(got_ref, combine_ref, hidden_ref, out_ref):
    rows, width = out_ref.shape
    n, span, _ = got_ref.shape
    mixed = dot(combine_ref[...], got_ref[...].reshape(n * span, 128), ((0,), (0,)))
    mixed = mixed[:64] + mixed[64:]
    for k in range(width // 128):
        at = slice(128 * k, 128 * (k + 1))
        out_ref[:, at] = (hidden_ref[:, at].astype(F32) + mixed[8 * k : 8 * k + rows]).astype(BF)


def on_device(
    queries,
    latent_cache,
    lengths,
    w_value,
    w_out,
    stream,
    norm_gain,
    expert_ids,
    gate_weights,
    w_gate,
    w_up,
    w_down,
):
    n_ctx = lax.axis_size("ctx")
    n_row = lax.axis_size("row")
    n_exp = lax.axis_size("exp")
    groups, heads, query_width = queries.shape
    block = latent_cache.shape[1]
    latent = w_value.shape[1]
    width = stream.shape[1]
    units = w_gate.shape[2]
    experts = n_row * n_exp
    slots = 2 * experts
    per = heads // n_ctx
    tiles = latent // 128
    span = groups * tiles * per + per

    vmem = pl.BlockSpec(memory_space=pltpu.VMEM)
    anywhere = pl.BlockSpec(memory_space=pl.ANY)
    gain = norm_gain.reshape(1, width)
    route, combine = call(
        routing,
        (shape_of((slots * 8, 64), BF), shape_of((slots * 8, 128), BF)),
        (expert_ids, gate_weights),
        (slots * 8 * 64 * 100, slots * 8 * 400),
        in_specs=[pl.BlockSpec(memory_space=pltpu.SMEM)] * 2,
    )
    sent = pl.pallas_call(
        attend,
        out_shape=shape_of((n_ctx, span, 128), BF),
        in_specs=[
            pl.BlockSpec(memory_space=pltpu.HBM),
            pl.BlockSpec(memory_space=pltpu.HBM),
            pl.BlockSpec(memory_space=pltpu.HBM),
        ],
        scratch_shapes=[
            pltpu.VMEM((groups, query_width, heads), BF),
            pltpu.VMEM((groups, query_width, block), BF),
            pltpu.SMEM((groups,), I32),
            pltpu.SemaphoreType.DMA((2, groups)),
            pltpu.SemaphoreType.DMA,
        ],
        cost_estimate=pl.CostEstimate(
            flops=2 * groups * heads * block * (query_width + latent),
            bytes_accessed=2 * groups * (block + heads) * query_width,
            transcendentals=groups * heads * block,
        ),
        compiler_params=pltpu.CompilerParams(vmem_limit_bytes=53 * MIB),
    )(lengths, jnp.swapaxes(queries, 1, 2), jnp.swapaxes(latent_cache, 1, 2))
    got = exchange(sent, "ctx")
    sent = call(
        merge,
        shape_of((n_exp, groups * tiles, 128), BF),
        (got,),
        (1 << 22, 1 << 20),
        scratch_shapes=[pltpu.VMEM((n_exp * groups * tiles, 128), F32)],
    )
    got = exchange(sent, "exp")
    sent = call(
        project,
        shape_of((n_exp, 2 * groups, D // 2), BF),
        (got, w_value, w_out),
        (2 * 128 * 256 * D // 2, 2 * 128 * D * 2),
        scratch_shapes=[
            pltpu.VMEM((n_exp * groups * tiles, 128), F32),
            pltpu.VMEM((n_exp * groups, 128), F32),
            pltpu.VMEM((2 * n_exp * groups, 128), F32),
            pltpu.VMEM((2 * n_exp * groups, 128), F32),
        ],
    )
    got = exchange(sent, "exp")
    sent = call(add_heads, shape_of((n_ctx, groups, width), BF), (got,), (1 << 20, 1 << 20))
    got = exchange(sent, "ctx")
    hidden, sent = call(
        dispatch,
        (shape_of((groups, width), BF), shape_of((experts, 16, 128), BF)),
        (got, stream, route, gain, w_up),
        (1 << 23, 1 << 19),
        in_specs=[vmem] * 3 + [anywhere] * 2,
        scratch_shapes=[pltpu.VMEM((64, 128), F32)],
    )
    got = exchange(sent, ("row", "exp"))
    sent = call(
        gate_up,
        shape_of((n_ctx, slots // n_ctx, 2 * units + 128), BF),
        (got, gain, w_gate, w_up),
        (4 * slots * width * units, 4 * width * units),
        scratch_shapes=[pltpu.VMEM((slots * 8, 128), F32)],
    )
    got = exchange(sent, "ctx")
    sent = call(activate, shape_of((n_ctx, slots // n_ctx, units), BF), (got,), (1 << 20, 1 << 19))
    got = exchange(sent, "ctx")
    sent = call(
        down,
        shape_of((experts, 16, 128), BF),
        (got, w_down),
        (2 * slots * width * units, 2 * width * units),
        scratch_shapes=[pltpu.VMEM((slots * 8, 128), F32)],
    )
    got = exchange(sent, ("row", "exp"))
    return call(
        combine_rows, shape_of((groups, width), BF), (got, combine, hidden), (1 << 24, 1 << 18)
    )


def solution(mesh):
    placed = (
        P(("row", "exp"), None, None),
        P(("row", "exp"), "ctx", None),
        P(("row", "exp")),
        P(("ctx", "exp"), None, None),
        P(("ctx", "exp"), None),
        P(("row", "exp"), "ctx"),
        P("ctx"),
        P(("row", "exp"), None),
        P(("row", "exp"), None),
        P(("row", "exp"), "ctx", None),
        P(("row", "exp"), "ctx", None),
        P(("row", "exp"), None, "ctx"),
    )
    return jax.shard_map(
        on_device, mesh=mesh, in_specs=placed, out_specs=P(("row", "exp"), "ctx"), check_vma=False
    )
```

```python
import functools

import jax
import jax.numpy as jnp
from jax import lax
from jax.experimental import pallas as pl
from jax.experimental.pallas import tpu as pltpu
from jax.sharding import PartitionSpec as P

D = 7168
QK_HEAD = 192
BF = jnp.bfloat16
F32 = jnp.float32
I32 = jnp.int32
epsilon = 1e-06
DEAD = -1e30
LOG2E = 1.4426950408889634
MIB = 1024 * 1024


def exchange(x, axes):
    return lax.all_to_all(x, axes, split_axis=0, concat_axis=0, tiled=True)


def dot(a, b, dims=((1,), (0,))):
    return lax.dot_general(a, b, (dims, ((), ())), preferred_element_type=F32)


def iota(shape, dim):
    return lax.broadcasted_iota(I32, shape, dim)


def pieces(x):
    hi = x.astype(BF).astype(F32)
    mid = (x - hi).astype(BF).astype(F32)
    low = (x - hi - mid).astype(BF).astype(F32)
    return hi, mid, low


def call(kernel, out, args, cost, **kw):
    return pl.pallas_call(
        kernel,
        out_shape=out,
        cost_estimate=pl.CostEstimate(flops=cost[0], bytes_accessed=cost[1], transcendentals=0),
        compiler_params=pltpu.CompilerParams(vmem_limit_bytes=24 * MIB),
        **kw,
    )(*args)


def shape_of(shape, dtype):
    return jax.ShapeDtypeStruct(shape, dtype)


def attend(length_hbm, q_hbm, kv_hbm, out_ref, q_ref, kv_ref, length_ref, sem, length_sem):
    rows, _, heads = q_ref.shape
    block = kv_ref.shape[2]
    n_ctx, span, _ = out_ref.shape
    per = heads // n_ctx
    tiles = (span - per) // per // rows
    latent = tiles * 128
    copies = []
    for r in range(rows):
        pair = (
            pltpu.make_async_copy(q_hbm.at[r], q_ref.at[r], sem.at[0, r]),
            pltpu.make_async_copy(kv_hbm.at[r], kv_ref.at[r], sem.at[1, r]),
        )
        for copy in pair:
            copy.start()
        copies.append(pair)
    length_copy = pltpu.make_async_copy(length_hbm, length_ref, length_sem)
    length_copy.start()
    length_copy.wait()
    first = lax.axis_index("ctx") * block
    lane = iota((heads, 128), 1)
    stat = jnp.zeros((heads, 128), F32)

    def products(r):
        for copy in copies[r]:
            copy.wait()
        return dot(q_ref[r], kv_ref[r], ((0,), (0,)))

    scale = QK_HEAD ** (-0.5)
    following = products(0)
    for r in range(rows):
        scores = following
        if r + 1 < rows:
            following = products(r + 1)
        live = iota((heads, block), 1) < length_ref[r] - first
        scores = jnp.where(live, scores, DEAD)
        top = jnp.max(scores, axis=1, keepdims=True)
        weights = jnp.exp2((scores - jnp.maximum(top, 0.5 * DEAD)) * (scale * LOG2E))
        total = jnp.sum(weights, axis=1, keepdims=True)
        safe = jnp.where(total > 0, total, 1.0)
        part = dot(weights.astype(BF), kv_ref[r, :latent, :], ((1,), (1,))) * (1.0 / safe)
        part = part.astype(BF)
        for p, piece in enumerate(pieces(top * scale + jnp.log(safe))):
            stat = jnp.where(lane == 4 * r + p, piece, stat)
        for c in range(n_ctx):
            for t in range(tiles):
                at = (r * tiles + t) * per
                out_ref[c, at : at + per, :] = part[per * c : per * (c + 1), 128 * t : 128 * (t + 1)]
    stat = stat.astype(BF)
    for c in range(n_ctx):
        out_ref[c, span - per :, :] = stat[per * c : per * (c + 1)]


def merge(got_ref, out_ref, scratch):
    n_ctx, span, _ = got_ref.shape
    per = out_ref.shape[0]
    rows = 4
    tiles = (span - per) // per // rows
    stat = got_ref[:, span - per :, :].astype(F32)
    lane = iota(stat.shape, 2)
    n = rows * tiles
    for r in range(rows):
        mine = (lane >= 4 * r) & (lane < 4 * r + 3)
        lse = jnp.sum(jnp.where(mine, stat, 0.0), axis=2, keepdims=True)
        factor = jnp.exp(lse - jnp.max(lse, axis=0, keepdims=True))
        factor = factor * (1.0 / jnp.sum(factor, axis=0, keepdims=True))
        for t in range(tiles):
            at = r * tiles + t
            part = got_ref[:, at * per : (at + 1) * per, :].astype(F32)
            scratch[pl.ds(at, per, stride=n), :] = jnp.sum(factor * part, axis=0)
    out_ref[...] = scratch[...].astype(BF).reshape(out_ref.shape)


def project(got_ref, wv_ref, wo_ref, out_ref, got_wide, values_wide, upper, lower):
    n_exp, n, _ = got_ref.shape
    rows = 4
    tiles = n // rows
    size = n_exp * n
    count = n_exp * rows
    got_wide[...] = got_ref[...].astype(F32).reshape(size, 128)
    values = jnp.zeros((count, wv_ref.shape[2]), F32)
    for t in range(tiles):
        latents = got_wide[pl.ds(t, count, stride=tiles), :].astype(BF)
        values += dot(latents, wv_ref[0, 128 * t : 128 * (t + 1), :])
    values_wide[...] = values
    upper[...] = jnp.zeros_like(upper)
    lower[...] = jnp.zeros_like(lower)
    for b in range(rows):
        line = values_wide[pl.ds(b, n_exp, stride=rows), :]
        upper[pl.ds(b, n_exp, stride=8), :] = line
        lower[pl.ds(rows + b, n_exp, stride=8), :] = line
    lhs = jnp.concatenate([upper[...], lower[...]], axis=1).astype(BF)
    half = wo_ref.shape[1] // 2
    step = 512
    for at in range(0, half, step):
        rhs = jnp.concatenate([wo_ref[:, at : at + step], wo_ref[:, half + at : half + at + step]], axis=0)
        out_ref[:, :, at : at + step] = dot(lhs, rhs).astype(BF).reshape(n_exp, 8, step)


def add_heads(got_ref, out_ref):
    n_ctx, rows, width = out_ref.shape
    per = n_ctx // 2
    for q in range(per):
        total = jnp.sum(got_ref[:, :, width * q : width * (q + 1)].astype(F32), axis=0)
        out_ref[q] = total[:rows].astype(BF)
        out_ref[per + q] = total[rows:].astype(BF)


def dispatch(got_ref, stream_ref, route_ref, gain_ref, later_ref, hidden_ref, out_ref, scratch):
    del gain_ref, later_ref
    rows, width = stream_ref.shape
    hidden = (stream_ref[...].astype(F32) + jnp.sum(got_ref[...].astype(F32), axis=0)).astype(BF)
    hidden_ref[...] = hidden
    wide = hidden.astype(F32)
    scratch[...] = jnp.zeros_like(scratch)
    for k in range(width // 128):
        scratch[8 * k : 8 * k + rows, :] = wide[:, 128 * k : 128 * (k + 1)]
    out_ref[...] = dot(route_ref[...], scratch[...].astype(BF)).astype(BF).reshape(out_ref.shape)


def routing(ids_ref, weights_ref, route_ref, combine_ref):
    size = route_ref.shape[0]
    rows, picks = ids_ref.shape
    i, j = iota((size, 64), 0), iota((size, 64), 1)
    expert, slot = i // 16, (i // 8) % 2
    same = (i % 8) == (j // 8)
    count = jnp.zeros((size, 64), I32)
    route = jnp.zeros((size, 64), F32)
    combine = jnp.zeros((size, 64), F32)
    for b in range(rows):
        weight = jnp.zeros((size, 64), F32)
        named = jnp.zeros((size, 64), I32)
        for k in range(picks):
            hit = expert == ids_ref[b, k]
            weight = jnp.where(hit, weights_ref[b, k], weight)
            named = jnp.where(hit, 1, named)
        mine = (named == 1) & (count == slot) & same & (j % 8 == b)
        route = jnp.where(mine, 1.0, route)
        combine = jnp.where(mine, weight, combine)
        count = count + named
    route_ref[...] = route.astype(BF)
    hi = combine.astype(BF)
    low = (combine - hi.astype(F32)).astype(BF)
    combine_ref[...] = jnp.concatenate([hi, low], axis=1)


def gate_up(got_ref, gain_ref, wg_ref, wu_ref, out_ref, scratch):
    n, span, _ = got_ref.shape
    slots = n * span // 8
    tiles = wg_ref.shape[1] // 128
    scratch[...] = got_ref[...].astype(F32).reshape(n * span, 128)
    sumsq = jnp.zeros((slots, 128), F32)
    scaled = []
    for k in range(tiles):
        part = scratch[pl.ds(k, slots, stride=8), :]
        sumsq += part * part
        scaled.append((part * gain_ref[:, 128 * k : 128 * (k + 1)]).astype(BF))
    scaled = jnp.concatenate(scaled, axis=1)
    units = wg_ref.shape[2]
    step = 512
    per = out_ref.shape[1]
    for w_ref, base in ((wg_ref, 0), (wu_ref, units)):
        for at in range(0, units, step):
            part = dot(scaled, w_ref[0, :, at : at + step]).astype(BF)
            out_ref[:, :, base + at : base + at + step] = part.reshape(slots // per, per, step)
    lane = iota((slots, 128), 1)
    stat = jnp.zeros((slots, 128), F32)
    for p, piece in enumerate(pieces(jnp.sum(sumsq, axis=1, keepdims=True))):
        stat = jnp.where(lane == p, piece, stat)
    out_ref[:, :, 2 * units :] = stat.astype(BF).reshape(slots // per, per, 128)


def activate(got_ref, out_ref):
    units = out_ref.shape[2]
    sums = jnp.sum(got_ref[...].astype(F32), axis=0)
    sumsq = jnp.sum(sums[:, 2 * units :], axis=1, keepdims=True)
    inverse = lax.rsqrt(sumsq / D + epsilon)
    gate = inverse * sums[:, :units]
    up = inverse * sums[:, units : 2 * units]
    active = (gate / (1.0 + jnp.exp(-gate)) * up).astype(BF)
    for c in range(out_ref.shape[0]):
        out_ref[c] = active


def down(got_ref, wd_ref, out_ref, scratch):
    n_ctx, per, units = got_ref.shape
    slots = n_ctx * per
    tiles = wd_ref.shape[2] // 128
    active = got_ref[...].reshape(slots, units)
    produced = dot(active, wd_ref[0])
    for k in range(tiles):
        scratch[pl.ds(k, slots, stride=8), :] = produced[:, 128 * k : 128 * (k + 1)]
    scratch[pl.ds(tiles, slots, stride=8), :] = jnp.zeros((slots, 128), F32)
    out_ref[...] = scratch[...].astype(BF).reshape(out_ref.shape)


def combine_rows(got_ref, combine_ref, hidden_ref, out_ref):
    rows, width = out_ref.shape
    n, span, _ = got_ref.shape
    mixed = dot(combine_ref[...], got_ref[...].reshape(n * span, 128), ((0,), (0,)))
    mixed = mixed[:64] + mixed[64:]
    for k in range(width // 128):
        at = slice(128 * k, 128 * (k + 1))
        out_ref[:, at] = (hidden_ref[:, at].astype(F32) + mixed[8 * k : 8 * k + rows]).astype(BF)


def on_device(
    queries,
    latent_cache,
    lengths,
    w_value,
    w_out,
    stream,
    norm_gain,
    expert_ids,
    gate_weights,
    w_gate,
    w_up,
    w_down,
):
    n_ctx = lax.axis_size("ctx")
    n_row = lax.axis_size("row")
    n_exp = lax.axis_size("exp")
    groups, heads, query_width = queries.shape
    block = latent_cache.shape[1]
    latent = w_value.shape[1]
    width = stream.shape[1]
    units = w_gate.shape[2]
    experts = n_row * n_exp
    slots = 2 * experts
    per = heads // n_ctx
    tiles = latent // 128
    span = groups * tiles * per + per

    vmem = pl.BlockSpec(memory_space=pltpu.VMEM)
    anywhere = pl.BlockSpec(memory_space=pl.ANY)
    gain = norm_gain.reshape(1, width)
    route, combine = call(
        routing,
        (shape_of((slots * 8, 64), BF), shape_of((slots * 8, 128), BF)),
        (expert_ids, gate_weights),
        (slots * 8 * 64 * 100, slots * 8 * 400),
        in_specs=[pl.BlockSpec(memory_space=pltpu.SMEM)] * 2,
    )
    sent = pl.pallas_call(
        attend,
        out_shape=shape_of((n_ctx, span, 128), BF),
        in_specs=[
            pl.BlockSpec(memory_space=pltpu.HBM),
            pl.BlockSpec(memory_space=pltpu.HBM),
            pl.BlockSpec(memory_space=pltpu.HBM),
        ],
        scratch_shapes=[
            pltpu.VMEM((groups, query_width, heads), BF),
            pltpu.VMEM((groups, query_width, block), BF),
            pltpu.SMEM((groups,), I32),
            pltpu.SemaphoreType.DMA((2, groups)),
            pltpu.SemaphoreType.DMA,
        ],
        cost_estimate=pl.CostEstimate(
            flops=2 * groups * heads * block * (query_width + latent),
            bytes_accessed=2 * groups * (block + heads) * query_width,
            transcendentals=groups * heads * block,
        ),
        compiler_params=pltpu.CompilerParams(vmem_limit_bytes=53 * MIB),
    )(lengths, jnp.swapaxes(queries, 1, 2), jnp.swapaxes(latent_cache, 1, 2))
    got = exchange(sent, "ctx")
    sent = call(
        merge,
        shape_of((n_exp, groups * tiles, 128), BF),
        (got,),
        (1 << 22, 1 << 20),
        scratch_shapes=[pltpu.VMEM((n_exp * groups * tiles, 128), F32)],
    )
    got = exchange(sent, "exp")
    sent = call(
        project,
        shape_of((n_exp, 2 * groups, D // 2), BF),
        (got, w_value, w_out),
        (2 * 128 * 256 * D // 2, 2 * 128 * D * 2),
        scratch_shapes=[
            pltpu.VMEM((n_exp * groups * tiles, 128), F32),
            pltpu.VMEM((n_exp * groups, 128), F32),
            pltpu.VMEM((2 * n_exp * groups, 128), F32),
            pltpu.VMEM((2 * n_exp * groups, 128), F32),
        ],
    )
    got = exchange(sent, "exp")
    sent = call(add_heads, shape_of((n_ctx, groups, width), BF), (got,), (1 << 20, 1 << 20))
    got = exchange(sent, "ctx")
    hidden, sent = call(
        dispatch,
        (shape_of((groups, width), BF), shape_of((experts, 16, 128), BF)),
        (got, stream, route, gain, w_up),
        (1 << 23, 1 << 19),
        in_specs=[vmem] * 3 + [anywhere] * 2,
        scratch_shapes=[pltpu.VMEM((64, 128), F32)],
    )
    got = exchange(sent, ("row", "exp"))
    sent = call(
        gate_up,
        shape_of((n_ctx, slots // n_ctx, 2 * units + 128), BF),
        (got, gain, w_gate, w_up),
        (4 * slots * width * units, 4 * width * units),
        scratch_shapes=[pltpu.VMEM((slots * 8, 128), F32)],
    )
    got = exchange(sent, "ctx")
    sent = call(activate, shape_of((n_ctx, slots // n_ctx, units), BF), (got,), (1 << 20, 1 << 19))
    got = exchange(sent, "ctx")
    sent = call(
        down,
        shape_of((experts, 16, 128), BF),
        (got, w_down),
        (2 * slots * width * units, 2 * width * units),
        scratch_shapes=[pltpu.VMEM((slots * 8, 128), F32)],
    )
    got = exchange(sent, ("row", "exp"))
    return call(
        combine_rows, shape_of((groups, width), BF), (got, combine, hidden), (1 << 24, 1 << 18)
    )


def solution(mesh):
    placed = (
        P(("row", "exp"), None, None),
        P(("row", "exp"), "ctx", None),
        P(("row", "exp")),
        P(("ctx", "exp"), None, None),
        P(("ctx", "exp"), None),
        P(("row", "exp"), "ctx"),
        P("ctx"),
        P(("row", "exp"), None),
        P(("row", "exp"), None),
        P(("row", "exp"), "ctx", None),
        P(("row", "exp"), "ctx", None),
        P(("row", "exp"), None, "ctx"),
    )
    return jax.shard_map(
        on_device, mesh=mesh, in_specs=placed, out_specs=P(("row", "exp"), "ctx"), check_vma=False
    )
```
